768 devices in a mesh: dp: 12 (over z_lo, core), node: 64 (over z_hi, y, x).
Axes of the slice: x: 4, y: 8, z: 12 (z_hi: 2, z_lo: 6; z = z_hi * 6 + z_lo), core: 2. Of those that a mesh axis runs over, the one named last changes fastest.
Arguments:
- tokens: bfloat16 [196608, 2048], P(('dp', 'node')), may hold values from -6 to 6
- key_cot: bfloat16 [196608, 256], P(('dp', 'node')), may hold values from -6 to 6
- value_cot: bfloat16 [196608, 256], P(('dp', 'node')), may hold values from -6 to 6
- key_mant: bfloat16 [2048, 256], P('node'), may hold values from -0.125 to 0.125
- value_mant: bfloat16 [2048, 256], P('node'), may hold values from -0.125 to 0.125
- key_expo: int32 [2048, 2], P('node'), may hold values from -2 to 1
- value_expo: int32 [2048, 2], P('node'), may hold values from -2 to 1
Outputs:
- keys: bfloat16 [196608, 256], P(('dp', 'node'))
- values: bfloat16 [196608, 256], P(('dp', 'node'))
- tokens_grad: bfloat16 [196608, 2048], P(('dp', 'node'))
- key_grad: float32 [2048, 256], P('node')
- value_grad: float32 [2048, 256], P('node')
The draws below stay inside these ranges and needn't reach their ends.
All inputs are finite; a program needn't handle non-finite values.
Results may differ from the reference program's by a relative error of at most 0.001.
Values may be sent and summed in bfloat16 or wider, within the bound.
A program may use at most 32 MiB of HBM per device.

```python
import math
import jax
import jax.numpy as jnp

D = 2048
BLOCK = 128
KVW = 256
TOKENS = 196608


def with_ends(result, key, smallest, top_value):
    extent = result.shape
    index_at = [jax.random.randint(jax.random.fold_in(key, axis), (), 0, extent[axis]) for axis in range(len(extent))]
    result = result.at[tuple(index_at)].set(smallest)
    longest = extent.index(max(extent))
    index_at[longest] = (index_at[longest] + 1) % extent[longest]
    return result.at[tuple(index_at)].set(top_value)


def block_scale(rng, dims, shards, least, largest):
    factor_of = 1.0
    for position, parts in shards:
        draws = jax.random.uniform(jax.random.fold_in(jax.random.fold_in(rng, 6), position), (parts,), jnp.float32, least / len(shards), largest / len(shards))
        factor_of = factor_of * jnp.repeat(jnp.exp(draws), dims[position] // parts).reshape((-1,) + (1,) * (len(dims) - 1 - position))
    return factor_of


def bell_draw(rng, dims, spread, bound, cuts=(), kind=jnp.bfloat16):
    loudness = block_scale(rng, dims, cuts, -0.22, 0.18) if cuts else 1.0
    entries = jax.random.normal(rng, dims, jnp.float32) * spread * loudness
    return jnp.minimum(jnp.maximum(entries, -bound), bound).astype(kind)


def setup_inputs(seed: int = 0) -> dict:
    key_list = jax.random.split(jax.random.key(seed), 8)
    return {
        "tokens": bell_draw(key_list[0], (TOKENS, D), 1.0, 6.0, ((0, 768),)),
        "key_cot": bell_draw(key_list[1], (TOKENS, KVW), 1.0, 6.0, ((0, 768),)),
        "value_cot": bell_draw(key_list[2], (TOKENS, KVW), 1.0, 6.0, ((0, 768),)),
        "key_mant": bell_draw(key_list[3], (D, KVW), D ** -0.5, 0.125, ((0, 64),)),
        "value_mant": bell_draw(key_list[4], (D, KVW), D ** -0.5, 0.125, ((0, 64),)),
        "key_expo": with_ends(jax.random.randint(key_list[5], (D, KVW // BLOCK), -2, 2), jax.random.fold_in(key_list[5], 1), -2, 1).astype(jnp.int32),
        "value_expo": with_ends(jax.random.randint(key_list[6], (D, KVW // BLOCK), -2, 2), jax.random.fold_in(key_list[6], 1), -2, 1).astype(jnp.int32),
    }


def dequant(mant, expo):
    factor = jnp.zeros(expo.shape, jnp.float32)
    for exponent in range(-2, 2):
        factor = factor + jnp.where(expo == exponent, jnp.float32(2.0 ** exponent), jnp.float32(0.0))
    blocks = mant.astype(jnp.float32).reshape(mant.shape[0], expo.shape[1], BLOCK)
    return (blocks * factor[:, :, None]).reshape(mant.shape).astype(jnp.bfloat16)

def reference(tokens, key_cot, value_cot, key_mant, value_mant, key_expo, value_expo):
    key_w = dequant(key_mant, key_expo)
    value_w = dequant(value_mant, value_expo)
    keys = jnp.dot(tokens, key_w, preferred_element_type=jnp.float32).astype(jnp.bfloat16)
    values = jnp.dot(tokens, value_w, preferred_element_type=jnp.float32).astype(jnp.bfloat16)
    tokens_grad = (jnp.dot(key_cot, key_w.T, preferred_element_type=jnp.float32) + jnp.dot(value_cot, value_w.T, preferred_element_type=jnp.float32)).astype(jnp.bfloat16)
    scale = jnp.float32(1.0 / math.sqrt(TOKENS))
    key_grad = jnp.dot(tokens.T, key_cot, preferred_element_type=jnp.float32) * scale
    value_grad = jnp.dot(tokens.T, value_cot, preferred_element_type=jnp.float32) * scale
    return (keys, values, tokens_grad, key_grad, value_grad)
```

```python
import math

import jax
import jax.numpy as jnp
from jax import lax
from jax.experimental import pallas as pl
from jax.experimental.pallas import tpu as pltpu
from jax.sharding import PartitionSpec as P

MESH = pl.DeviceIdType.MESH
F32, BF16, I16 = jnp.float32, jnp.bfloat16, jnp.int16
NX, NY, NZ = 4, 8, 12
HALF = NZ // 2
ROWS = 32
COLS = 512
TOK = 256
DH = 1024
REDUCERS = 4
STEPS = 32766.0
TINY = 1e-30


def coordinates():
    dp, node = lax.axis_index("dp"), lax.axis_index("node")
    x = lax.rem(node, NX)
    y = lax.rem(node // NX, NY)
    half = node // (NX * NY)
    low = dp // 2
    core = lax.rem(dp, 2)
    return x, y, half, low, core


def device(x, y, z, core):
    return {
        "dp": lax.rem(z, HALF) * 2 + core,
        "node": (z // HALF) * (NX * NY) + y * NX + x,
    }


def shard_rows(mant, expo_t):
    factor = jnp.zeros(expo_t.shape, F32)
    for exponent in range(-2, 2):
        factor = factor + jnp.where(expo_t == exponent, F32(2.0**exponent), F32(0.0))
    parts = []
    for block in range(2):
        spread = lax.dot_general(
            factor[block : block + 1, :],
            jnp.ones((1, 128), F32),
            (((0,), (0,)), ((), ())),
            preferred_element_type=F32,
        )
        parts.append(mant[:, block * 128 : (block + 1) * 128].astype(F32) * spread)
    return jnp.concatenate(parts, axis=1).astype(BF16)


def over_rows(left, right):
    return lax.dot_general(left, right, (((0,), (0,)), ((), ())), preferred_element_type=F32)


def over_cols(left, right):
    return lax.dot_general(left, right, (((1,), (1,)), ((), ())), preferred_element_type=F32)


def kernel(
    tokens, key_cot, value_cot, key_mant, value_mant, key_expo, value_expo,
    keys, values, tokens_grad, key_grad, value_grad,
    tok, tok2, cot, cot2, mant, expo, part, codes, peaks, codes_in, peaks_in,
    sums, sums_in, total, total_in, final, own_w, other_w, tgrad, kv,
    load_sem, store_sem, send_c, recv_c, send_x, recv_x, send_y, recv_y,
    send_z, recv_z, send_g, recv_g, send_wz, recv_wz, send_wy, recv_wy, send_wx, recv_wx,
):
    x, y, half, low, core = coordinates()
    z = half * HALF + low
    sibling = device(x, y, z, 1 - core)
    home = core == half
    mine = pl.multiple_of(core * DH, DH)
    theirs = pl.multiple_of((1 - core) * DH, DH)

    def remote(src, dst, send, recv, to):
        return pltpu.make_async_remote_copy(
            src_ref=src, dst_ref=dst, send_sem=send, recv_sem=recv, device_id=to, device_id_type=MESH
        )

    loads = [
        pltpu.make_async_copy(key_mant, mant.at[0], load_sem.at[0]),
        pltpu.make_async_copy(value_mant, mant.at[1], load_sem.at[1]),
        pltpu.make_async_copy(key_expo, expo.at[0], load_sem.at[2]),
        pltpu.make_async_copy(value_expo, expo.at[1], load_sem.at[3]),
        pltpu.make_async_copy(tokens, tok, load_sem.at[4]),
        pltpu.make_async_copy(key_cot, cot.at[:, pl.ds(0, 256)], load_sem.at[5]),
        pltpu.make_async_copy(value_cot, cot.at[:, pl.ds(256, 256)], load_sem.at[6]),
    ]
    for load in loads:
        load.start()

    barrier = pltpu.get_barrier_semaphore()

    def greet(to):
        pl.semaphore_signal(barrier, inc=1, device_id=to, device_id_type=MESH)

    for d in range(1, NZ):
        greet(device(x, y, lax.rem(z + d, NZ), core))
    for d in range(1, NY):
        greet(device(x, lax.rem(y + d, NY), z, core))
    for d in range(1, NX):
        greet(device(lax.rem(x + d, NX), y, z, core))
    greet(sibling)

    for load in loads[:4]:
        load.wait()

    @pl.when(home)
    def _():
        own_w[y, x, :, 0:256] = shard_rows(mant[0], expo[0])
        own_w[y, x, :, 256:512] = shard_rows(mant[1], expo[1])

    for load in loads[4:]:
        load.wait()

    def own_part(j, _):
        left = tok[:, pl.ds(pl.multiple_of(mine + j * 128, 128), 128)]
        part[j] = over_rows(left, cot[...]).reshape(NX, ROWS, COLS)
        return 0

    lax.fori_loop(0, NY, own_part, 0)
    pl.semaphore_wait(barrier, (NZ - 1) + (NY - 1) + (NX - 1) + 1)

    swap_tok = remote(tok.at[:, pl.ds(theirs, DH)], tok2, send_c.at[0], recv_c.at[0], sibling)
    swap_cot = remote(cot, cot2, send_c.at[1], recv_c.at[1], sibling)
    swap_tok.start()
    swap_cot.start()

    across = device(x, y, lax.rem(z + HALF, NZ), core)
    w_z = remote(own_w.at[y, x], own_w.at[y, x], send_wz, recv_wz, across)

    @pl.when(home)
    def _():
        w_z.start()

    swap_tok.wait_recv()
    swap_cot.wait_recv()

    def encode(j, _):
        left = tok2[:, pl.ds(pl.multiple_of(j * 128, 128), 128)]
        part[j] = part[j] + over_rows(left, cot2[...]).reshape(NX, ROWS, COLS)
        for d in range(1, NX):
            chunk = part[j, lax.rem(x + d, NX)]
            peak = jnp.maximum(jnp.max(jnp.abs(chunk), axis=0, keepdims=True), TINY)
            codes[d - 1, j] = jnp.round(chunk * (STEPS / peak)).astype(jnp.int32).astype(I16)
            peaks[d - 1, j] = jnp.broadcast_to(peak * (1.0 / STEPS), (8, COLS))
        return 0

    def x_copies(part_of, d):
        to = device(lax.rem(x + d, NX), y, z, core)
        blocks = pl.ds(part_of * 4, 4)
        return (
            remote(codes.at[d - 1, blocks], codes_in.at[d - 1, blocks],
                   send_x.at[0, part_of, d - 1], recv_x.at[0, part_of, d - 1], to),
            remote(peaks.at[d - 1, blocks], peaks_in.at[d - 1, blocks],
                   send_x.at[1, part_of, d - 1], recv_x.at[1, part_of, d - 1], to),
        )

    for part_of in range(2):
        lax.fori_loop(part_of * 4, part_of * 4 + 4, encode, 0)
        for d in (2, 1, 3):
            for copy in x_copies(part_of, d):
                copy.start()

    @pl.when(jnp.logical_not(home))
    def _():
        w_z.wait_recv()

    def w_y(d, block):
        to = device(x, lax.rem(y + d, NY), z, core)
        return remote(own_w.at[block, x], own_w.at[block, x], send_wy.at[d - 1], recv_wy.at[d - 1], to)

    for d in (4, 3, 5, 2, 6, 1, 7):
        w_y(d, y).start()

    def add_x(j, _):
        value = part[j, x]
        for d in range(1, NX):
            scale = peaks_in[d - 1, j][0:1, :]
            value = value + codes_in[d - 1, j].astype(jnp.int32).astype(F32) * scale
        sums[j] = value
        return 0

    def y_copy(d, block):
        to = device(x, lax.rem(y + d, NY), z, core)
        return remote(sums.at[block], sums_in.at[d - 1], send_y.at[d - 1], recv_y.at[d - 1], to)

    for part_of in range(2):
        for d in (2, 1, 3):
            for copy in x_copies(part_of, d):
                copy.wait_recv()
        lax.fori_loop(part_of * 4, part_of * 4 + 4, add_x, 0)
        for d in (4, 3, 5, 2, 6, 1, 7):
            block = lax.rem(y + d, NY)

            @pl.when(block // 4 == part_of)
            def _(d=d, block=block):
                y_copy(d, block).start()

    for d in range(1, NY):
        w_y(d, lax.rem(y + NY - d, NY)).wait_recv()

    def w_x(d, column):
        to = device(lax.rem(x + d, NX), y, z, core)
        return remote(own_w.at[:, column], own_w.at[:, column], send_wx.at[d - 1], recv_wx.at[d - 1], to)

    for d in (2, 1, 3):
        w_x(d, x).start()

    for d in range(1, NY):
        y_copy(d, y).wait_recv()
    value = sums[y]
    for d in range(1, NY):
        value = value + sums_in[d - 1]
    total[...] = value.reshape(REDUCERS, 8, COLS)

    def z_copy(j, slot):
        to = device(x, y, core * HALF + 1 + j, core)
        return remote(total.at[j], total_in.at[slot], send_z.at[j], recv_z.at[slot], to)

    for j in range(REDUCERS):

        @pl.when(z != core * HALF + 1 + j)
        def _(j=j):
            z_copy(j, z).start()

    for d in range(1, NX):
        w_x(d, lax.rem(x + NX - d, NX)).wait_recv()
    w_c = remote(own_w, other_w, send_c.at[2], recv_c.at[2], sibling)
    w_c.start()
    weights = own_w[...].reshape(DH, COLS)
    kv[...] = jnp.dot(tok[:, pl.ds(mine, DH)], weights, preferred_element_type=F32)
    tgrad[core] = over_cols(cot[...], weights).astype(BF16)
    out_mine = pltpu.make_async_copy(tgrad.at[core], tokens_grad.at[:, pl.ds(mine, DH)], store_sem.at[0])
    out_mine.start()

    reducer = jnp.logical_and(home, jnp.logical_and(low >= 1, low <= REDUCERS))
    scale = F32(1.0 / math.sqrt(NX * NY * NZ * 2 * TOK))

    def g_copy(row, d):
        to = device(x, y, half * HALF + lax.rem(low + d, HALF), core)
        return remote(final.at[row], final.at[row], send_g.at[d - 1], recv_g.at[row], to)

    @pl.when(reducer)
    def _():
        for d in range(1, NZ):
            z_copy(0, lax.rem(z + d, NZ)).wait_recv()
        value = total[low - 1]
        for d in range(1, NZ):
            value = value + total_in[lax.rem(z + d, NZ)]
        final[low - 1] = value * scale
        for d in (3, 2, 4, 1, 5):
            g_copy(low - 1, d).start()

    w_c.wait_recv()
    weights = other_w[...].reshape(DH, COLS)
    both = kv[...] + jnp.dot(tok[:, pl.ds(theirs, DH)], weights, preferred_element_type=F32)
    tgrad[1 - core] = over_cols(cot[...], weights).astype(BF16)
    out_theirs = pltpu.make_async_copy(
        tgrad.at[1 - core], tokens_grad.at[:, pl.ds(theirs, DH)], store_sem.at[1]
    )
    out_theirs.start()
    kv_out = pl.ds(0, 256), pl.ds(256, 256)
    codes_kv = both.astype(BF16)
    cot2[...] = codes_kv
    out_keys = pltpu.make_async_copy(cot2.at[:, kv_out[0]], keys, store_sem.at[2])
    out_values = pltpu.make_async_copy(cot2.at[:, kv_out[1]], values, store_sem.at[3])
    out_keys.start()
    out_values.start()

    final_c = remote(final, final, send_c.at[3], recv_c.at[3], sibling)

    @pl.when(home)
    def _():
        for j in range(REDUCERS):

            @pl.when(low != 1 + j)
            def _(j=j):
                g_copy(j, 1).wait_recv()

        final_c.start()
        final_c.wait_send()

    @pl.when(jnp.logical_not(home))
    def _():
        final_c.wait_recv()

    for part_index, out in ((0, key_grad), (1, value_grad)):
        for j in range(REDUCERS):
            pltpu.make_async_copy(
                final.at[j, :, kv_out[part_index]], out.at[pl.ds(8 * j, 8)], store_sem.at[4 + part_index * 4 + j]
            ).start()

    swap_tok.wait_send()
    swap_cot.wait_send()

    @pl.when(home)
    def _():
        w_z.wait_send()

    for part_of in range(2):
        for d in range(1, NX):
            for copy in x_copies(part_of, d):
                copy.wait_send()
    for d in range(1, NY):
        w_y(d, y).wait_send()
        y_copy(d, y).wait_send()
    for d in range(1, NX):
        w_x(d, x).wait_send()
    w_c.wait_send()
    for j in range(REDUCERS):

        @pl.when(z != core * HALF + 1 + j)
        def _(j=j):
            z_copy(j, z).wait_send()

    @pl.when(reducer)
    def _():
        for d in range(1, HALF):
            g_copy(low - 1, d).wait_send()

    out_mine.wait()
    out_theirs.wait()
    out_keys.wait()
    out_values.wait()
    for part_index, out in ((0, key_grad), (1, value_grad)):
        for j in range(REDUCERS):
            pltpu.make_async_copy(
                final.at[j, :, kv_out[part_index]], out.at[pl.ds(8 * j, 8)], store_sem.at[4 + part_index * 4 + j]
            ).wait()


def on_device(tokens, key_cot, value_cot, key_mant, value_mant, key_expo, value_expo):
    dma, regular = pltpu.SemaphoreType.DMA, pltpu.SemaphoreType.REGULAR
    shape = jax.ShapeDtypeStruct
    anywhere = pl.BlockSpec(memory_space=pl.ANY)
    return pl.pallas_call(
        kernel,
        out_shape=(
            shape((TOK, 256), BF16),
            shape((TOK, 256), BF16),
            shape((TOK, 2 * DH), BF16),
            shape((ROWS, 256), F32),
            shape((ROWS, 256), F32),
        ),
        in_specs=[pl.BlockSpec(memory_space=pltpu.HBM)] * 7,
        out_specs=(anywhere,) * 5,
        scratch_shapes=[
            pltpu.VMEM((TOK, 2 * DH), BF16),
            pltpu.VMEM((TOK, DH), BF16),
            pltpu.VMEM((TOK, COLS), BF16),
            pltpu.VMEM((TOK, COLS), BF16),
            pltpu.VMEM((2, ROWS, 256), BF16),
            pltpu.VMEM((2, 2, ROWS), jnp.int32),
            pltpu.VMEM((NY, NX, ROWS, COLS), F32),
            pltpu.VMEM((NX - 1, NY, ROWS, COLS), I16),
            pltpu.VMEM((NX - 1, NY, 8, COLS), F32),
            pltpu.VMEM((NX - 1, NY, ROWS, COLS), I16),
            pltpu.VMEM((NX - 1, NY, 8, COLS), F32),
            pltpu.VMEM((NY, ROWS, COLS), F32),
            pltpu.VMEM((NY - 1, ROWS, COLS), F32),
            pltpu.VMEM((REDUCERS, 8, COLS), F32),
            pltpu.VMEM((NZ, 8, COLS), F32),
            pltpu.VMEM((REDUCERS, 8, COLS), F32),
            pltpu.VMEM((NY, NX, ROWS, COLS), BF16),
            pltpu.VMEM((NY, NX, ROWS, COLS), BF16),
            pltpu.VMEM((2, TOK, DH), BF16),
            pltpu.VMEM((TOK, COLS), F32),
            dma((7,)),
            dma((12,)),
            dma((4,)), dma((4,)),
            dma((2, 2, NX - 1)), dma((2, 2, NX - 1)),
            dma((NY - 1,)), dma((NY - 1,)),
            dma((REDUCERS,)), dma((NZ,)),
            dma((HALF - 1,)), dma((REDUCERS,)),
            dma, dma,
            dma((NY - 1,)), dma((NY - 1,)),
            dma((NX - 1,)), dma((NX - 1,)),
        ],
        compiler_params=pltpu.CompilerParams(
            collective_id=0, has_side_effects=True, vmem_limit_bytes=64 * 1024 * 1024
        ),
        name="projections",
    )(tokens, key_cot, value_cot, key_mant, value_mant, key_expo.T, value_expo.T)


def solution(mesh):
    rows, owned = P(("dp", "node"), None), P("node", None)
    return jax.shard_map(
        on_device,
        mesh=mesh,
        in_specs=(rows, rows, rows, owned, owned, owned, owned),
        out_specs=(rows, rows, rows, owned, owned),
        check_vma=False,
    )
```

```python
import math

import jax
import jax.numpy as jnp
from jax import lax
from jax.experimental import pallas as pl
from jax.experimental.pallas import tpu as pltpu
from jax.sharding import PartitionSpec as P

MESH = pl.DeviceIdType.MESH
F32, BF16, I16 = jnp.float32, jnp.bfloat16, jnp.int16
NX, NY, NZ = 4, 8, 12
HALF = NZ // 2
ROWS = 32
KVW = 256
COLS = 2 * KVW
TOK = 256
DH = 1024
REDUCERS = 4
STEPS = 32766.0
TINY = 1e-30


def coordinates():
    dp, node = lax.axis_index("dp"), lax.axis_index("node")
    x = lax.rem(node, NX)
    y = lax.rem(node // NX, NY)
    half = node // (NX * NY)
    low = dp // 2
    core = lax.rem(dp, 2)
    return x, y, half, low, core


def device(x, y, z, core):
    return {
        "dp": lax.rem(z, HALF) * 2 + core,
        "node": (z // HALF) * (NX * NY) + y * NX + x,
    }


def shard_rows(mant, expo_t):
    factor = jnp.zeros(expo_t.shape, F32)
    for exponent in range(-2, 2):
        factor = factor + jnp.where(expo_t == exponent, F32(2.0**exponent), F32(0.0))
    parts = []
    for block in range(2):
        spread = lax.dot_general(
            factor[block : block + 1, :],
            jnp.ones((1, 128), F32),
            (((0,), (0,)), ((), ())),
            preferred_element_type=F32,
        )
        parts.append(mant[:, block * 128 : (block + 1) * 128].astype(F32) * spread)
    return jnp.concatenate(parts, axis=1).astype(BF16)


def over_rows(left, right):
    return lax.dot_general(left, right, (((0,), (0,)), ((), ())), preferred_element_type=F32)


def over_cols(left, right):
    return lax.dot_general(left, right, (((1,), (1,)), ((), ())), preferred_element_type=F32)


def kernel(
    tokens, key_cot, value_cot, key_mant, value_mant, key_expo, value_expo,
    keys, values, tokens_grad, key_grad, value_grad,
    tok, tok2, cot, cot2, mant, expo, part, codes, peaks, codes_in, peaks_in,
    sums, sums_in, total, total_in, final, own_w, other_w, tgrad, kv, kv_out,
    load_sem, store_sem, send_c, recv_c, send_x, recv_x, send_y, recv_y,
    send_z, recv_z, send_g, recv_g, send_wz, recv_wz, send_wy, recv_wy, send_wx, recv_wx,
):
    x, y, half, low, core = coordinates()
    z = half * HALF + low
    sibling = device(x, y, z, 1 - core)
    home = core == half
    mine = pl.multiple_of(core * DH, DH)
    theirs = pl.multiple_of((1 - core) * DH, DH)

    def remote(src, dst, send, recv, to):
        return pltpu.make_async_remote_copy(
            src_ref=src, dst_ref=dst, send_sem=send, recv_sem=recv, device_id=to, device_id_type=MESH
        )

    loads = [
        pltpu.make_async_copy(key_mant, mant.at[0], load_sem.at[0]),
        pltpu.make_async_copy(value_mant, mant.at[1], load_sem.at[1]),
        pltpu.make_async_copy(key_expo, expo.at[0], load_sem.at[2]),
        pltpu.make_async_copy(value_expo, expo.at[1], load_sem.at[3]),
        pltpu.make_async_copy(tokens, tok, load_sem.at[4]),
        pltpu.make_async_copy(key_cot, cot.at[0], load_sem.at[5]),
        pltpu.make_async_copy(value_cot, cot.at[1], load_sem.at[6]),
    ]
    for load in loads:
        load.start()

    barrier = pltpu.get_barrier_semaphore()

    def greet(to):
        pl.semaphore_signal(barrier, inc=1, device_id=to, device_id_type=MESH)

    for d in (6, 5, 7, 4, 8, 3, 9, 2, 10, 1, 11):
        greet(device(x, y, lax.rem(z + d, NZ), core))
    for d in (4, 3, 5, 2, 6, 1, 7):
        greet(device(x, lax.rem(y + d, NY), z, core))
    for d in (2, 1, 3):
        greet(device(lax.rem(x + d, NX), y, z, core))
    greet(sibling)

    for load in loads[:4]:
        load.wait()

    @pl.when(home)
    def _():
        own_w[y, x, :, 0:KVW] = shard_rows(mant[0], expo[0])
        own_w[y, x, :, KVW:COLS] = shard_rows(mant[1], expo[1])

    for load in loads[4:]:
        load.wait()

    def own_part(b, _):
        left = tok[:, pl.ds(pl.multiple_of(b * 128, 128), 128)]
        part[b] = over_rows(left, cot[core]).reshape(NX, ROWS, KVW)
        return 0

    lax.fori_loop(0, 2 * NY, own_part, 0)
    pl.semaphore_wait(barrier, (NZ - 1) + (NY - 1) + (NX - 1) + 1)

    swap_cot = remote(cot.at[1 - core], cot2, send_c.at[0], recv_c.at[0], sibling)
    swaps = [
        remote(tok.at[:, pl.ds(h * DH, DH)], tok2.at[h], send_c.at[1 + h], recv_c.at[1 + h], sibling)
        for h in range(2)
    ]
    swap_cot.start()
    for swap in swaps:
        swap.start()

    across = device(x, y, lax.rem(z + HALF, NZ), core)
    w_z = remote(own_w.at[y, x], own_w.at[y, x], send_wz, recv_wz, across)

    @pl.when(home)
    def _():
        w_z.start()

    def x_copies(h, d):
        to = device(lax.rem(x + d, NX), y, z, core)
        return (
            remote(codes.at[h, d - 1], codes_in.at[h, d - 1],
                   send_x.at[0, h, d - 1], recv_x.at[0, h, d - 1], to),
            remote(peaks.at[h, d - 1], peaks_in.at[h, d - 1],
                   send_x.at[1, h, d - 1], recv_x.at[1, h, d - 1], to),
        )

    swap_cot.wait_recv()
    for h in range(2):
        swaps[h].wait_recv()

        def encode(j, _, h=h):
            left = tok2[h, :, pl.ds(pl.multiple_of(j * 128, 128), 128)]
            b = h * NY + j
            part[b] = part[b] + over_rows(left, cot2[...]).reshape(NX, ROWS, KVW)
            for d in range(1, NX):
                chunk = part[b, lax.rem(x + d, NX)]
                peak = jnp.maximum(jnp.max(jnp.abs(chunk), axis=0, keepdims=True), TINY)
                codes[h, d - 1, j] = jnp.round(chunk * (STEPS / peak)).astype(jnp.int32).astype(I16)
                peaks[h, d - 1, pl.ds(j, 1), :] = peak * (1.0 / STEPS)
            return 0

        lax.fori_loop(0, NY, encode, 0)
        for d in (2, 1, 3):
            for copy in x_copies(h, d):
                copy.start()

    @pl.when(jnp.logical_not(home))
    def _():
        w_z.wait_recv()

    def w_y(d, block):
        to = device(x, lax.rem(y + d, NY), z, core)
        return remote(own_w.at[block, x], own_w.at[block, x], send_wy.at[d - 1], recv_wy.at[d - 1], to)

    for d in (4, 3, 5, 2, 6, 1, 7):
        w_y(d, y).start()

    def y_copy(h, d, block):
        to = device(x, lax.rem(y + d, NY), z, core)
        return remote(sums.at[h, block], sums_in.at[h, d - 1], send_y.at[h, d - 1], recv_y.at[h, d - 1], to)

    for h in range(2):
        for d in (2, 1, 3):
            for copy in x_copies(h, d):
                copy.wait_recv()

        def add_x(j, _, h=h):
            value = part[h * NY + j, x]
            for d in range(1, NX):
                scale = peaks_in[h, d - 1, pl.ds(j, 1), :]
                value = value + codes_in[h, d - 1, j].astype(jnp.int32).astype(F32) * scale
            sums[h, j] = value
            return 0

        lax.fori_loop(0, NY, add_x, 0)
        for d in (4, 3, 5, 2, 6, 1, 7):
            y_copy(h, d, lax.rem(y + d, NY)).start()

    for d in range(1, NY):
        w_y(d, lax.rem(y + NY - d, NY)).wait_recv()

    def w_x(d, column):
        to = device(lax.rem(x + d, NX), y, z, core)
        return remote(own_w.at[:, column], own_w.at[:, column], send_wx.at[d - 1], recv_wx.at[d - 1], to)

    for d in (2, 1, 3):
        w_x(d, x).start()

    scale = F32(1.0 / math.sqrt(NX * NY * NZ * 2 * TOK))
    reducing = jnp.logical_and(low >= 1, low <= REDUCERS)

    def z_copy(h, j, slot):
        to = device(x, y, h * HALF + 1 + j, core)
        return remote(total.at[h, j], total_in.at[slot], send_z.at[h, j], recv_z.at[slot], to)

    def rows_of(j):
        return pl.ds(pl.multiple_of(8 * j, 8), 8)

    def g_copy(row, d):
        to = device(x, y, half * HALF + lax.rem(low + d, HALF), core)
        rows = final.at[core, rows_of(row)]
        return remote(rows, rows, send_g.at[d - 1], recv_g.at[row], to)

    def send_sums(h):
        for d in range(1, NY):
            y_copy(h, d, y).wait_recv()
        value = sums[h, y]
        for d in range(1, NY):
            value = value + sums_in[h, d - 1]
        total[h] = value.reshape(REDUCERS, 8, KVW)
        for j in range(REDUCERS):

            @pl.when(z != h * HALF + 1 + j)
            def _(j=j):
                z_copy(h, j, z).start()

    def reduce_sums(h):
        @pl.when(jnp.logical_and(half == h, reducing))
        def _():
            for d in range(1, NZ):
                z_copy(h, 0, lax.rem(z + d, NZ)).wait_recv()
            value = total[h, low - 1]
            for d in range(1, NZ):
                value = value + total_in[lax.rem(z + d, NZ)]
            final[core, rows_of(low - 1), :] = value * scale
            for d in (3, 2, 4, 1, 5):
                g_copy(low - 1, d).start()

    send_sums(0)
    reduce_sums(0)
    send_sums(1)

    for d in range(1, NX):
        w_x(d, lax.rem(x + NX - d, NX)).wait_recv()
    w_c = remote(own_w, other_w, send_c.at[3], recv_c.at[3], sibling)
    w_c.start()

    def products(weights, which, columns, store):
        grad = over_cols(cot[0], weights[:, 0:KVW]) + over_cols(cot[1], weights[:, KVW:COLS])
        tgrad[which] = grad.astype(BF16)
        out = pltpu.make_async_copy(tgrad.at[which], tokens_grad.at[:, pl.ds(columns, DH)], store_sem.at[store])
        out.start()
        return out, jnp.dot(tok[:, pl.ds(columns, DH)], weights, preferred_element_type=F32)

    out_mine, kv[...] = products(own_w[...].reshape(DH, COLS), core, mine, 0)
    reduce_sums(1)
    w_c.wait_recv()
    out_theirs, rest = products(other_w[...].reshape(DH, COLS), 1 - core, theirs, 1)
    kv_out[...] = (kv[...] + rest).astype(BF16)
    outs = [
        pltpu.make_async_copy(kv_out.at[:, pl.ds(0, KVW)], keys, store_sem.at[2]),
        pltpu.make_async_copy(kv_out.at[:, pl.ds(KVW, KVW)], values, store_sem.at[3]),
    ]
    for out in outs:
        out.start()

    for j in range(REDUCERS):

        @pl.when(low != 1 + j)
        def _(j=j):
            g_copy(j, 1).wait_recv()

    final_c = remote(final.at[core], final.at[core], send_c.at[4], recv_c.at[4], sibling)
    final_c.start()
    remote(final.at[1 - core], final.at[1 - core], send_c.at[4], recv_c.at[4], sibling).wait_recv()
    outs += [
        pltpu.make_async_copy(final.at[0], key_grad, store_sem.at[4]),
        pltpu.make_async_copy(final.at[1], value_grad, store_sem.at[5]),
    ]
    for out in outs[2:]:
        out.start()

    swap_cot.wait_send()
    for swap in swaps:
        swap.wait_send()

    @pl.when(home)
    def _():
        w_z.wait_send()

    for h in range(2):
        for d in range(1, NX):
            for copy in x_copies(h, d):
                copy.wait_send()
        for d in range(1, NY):
            y_copy(h, d, y).wait_send()
        for j in range(REDUCERS):

            @pl.when(z != h * HALF + 1 + j)
            def _(h=h, j=j):
                z_copy(h, j, z).wait_send()

    for d in range(1, NY):
        w_y(d, y).wait_send()
    for d in range(1, NX):
        w_x(d, x).wait_send()
    w_c.wait_send()

    @pl.when(reducing)
    def _():
        for d in range(1, HALF):
            g_copy(low - 1, d).wait_send()

    final_c.wait_send()
    out_mine.wait()
    out_theirs.wait()
    for out in outs:
        out.wait()


def place(*refs):
    sources, outs, staged, sems = refs[:5], refs[5:10], refs[10:15], refs[15]
    pieces = [(2, pl.ds(i * 64, 64)) for i in range(4)]
    pieces += [(i, pl.ds(0, sources[i].shape[0])) for i in (0, 1, 3, 4)]
    loads = [
        pltpu.make_async_copy(sources[i].at[rows], staged[i].at[rows], sems.at[0, k])
        for k, (i, rows) in enumerate(pieces)
    ]
    stores = [
        pltpu.make_async_copy(staged[i].at[rows], outs[i].at[rows], sems.at[1, k])
        for k, (i, rows) in enumerate(pieces)
    ]
    for load in loads:
        load.start()
    for load, store in zip(loads, stores):
        load.wait()
        store.start()
    for store in stores:
        store.wait()


def on_device(tokens, key_cot, value_cot, key_mant, value_mant, key_expo, value_expo):
    dma = pltpu.SemaphoreType.DMA
    shape = jax.ShapeDtypeStruct
    anywhere = pl.BlockSpec(memory_space=pl.ANY)
    results = (
        shape((TOK, KVW), BF16),
        shape((TOK, KVW), BF16),
        shape((TOK, 2 * DH), BF16),
        shape((ROWS, KVW), F32),
        shape((ROWS, KVW), F32),
    )
    outs = pl.pallas_call(
        kernel,
        out_shape=results,
        in_specs=[anywhere] * 7,
        out_specs=(anywhere,) * 5,
        scratch_shapes=[
            pltpu.VMEM((TOK, 2 * DH), BF16),
            pltpu.VMEM((2, TOK, DH), BF16),
            pltpu.VMEM((2, TOK, KVW), BF16),
            pltpu.VMEM((TOK, KVW), BF16),
            pltpu.VMEM((2, ROWS, KVW), BF16),
            pltpu.VMEM((2, 2, ROWS), jnp.int32),
            pltpu.VMEM((2 * NY, NX, ROWS, KVW), F32),
            pltpu.VMEM((2, NX - 1, NY, ROWS, KVW), I16),
            pltpu.VMEM((2, NX - 1, NY, KVW), F32),
            pltpu.VMEM((2, NX - 1, NY, ROWS, KVW), I16),
            pltpu.VMEM((2, NX - 1, NY, KVW), F32),
            pltpu.VMEM((2, NY, ROWS, KVW), F32),
            pltpu.VMEM((2, NY - 1, ROWS, KVW), F32),
            pltpu.VMEM((2, REDUCERS, 8, KVW), F32),
            pltpu.VMEM((NZ, 8, KVW), F32),
            pltpu.VMEM((2, ROWS, KVW), F32),
            pltpu.VMEM((NY, NX, ROWS, COLS), BF16),
            pltpu.VMEM((NY, NX, ROWS, COLS), BF16),
            pltpu.VMEM((2, TOK, DH), BF16),
            pltpu.VMEM((TOK, COLS), F32),
            pltpu.VMEM((TOK, COLS), BF16),
            dma((7,)),
            dma((6,)),
            dma((5,)), dma((5,)),
            dma((2, 2, NX - 1)), dma((2, 2, NX - 1)),
            dma((2, NY - 1)), dma((2, NY - 1)),
            dma((2, REDUCERS)), dma((NZ,)),
            dma((HALF - 1,)), dma((REDUCERS,)),
            dma, dma,
            dma((NY - 1,)), dma((NY - 1,)),
            dma((NX - 1,)), dma((NX - 1,)),
        ],
        compiler_params=pltpu.CompilerParams(
            collective_id=0, has_side_effects=True, vmem_limit_bytes=64 * 1024 * 1024
        ),
        name="projections",
    )(tokens, key_cot, value_cot, key_mant, value_mant, key_expo.T, value_expo.T)
    return pl.pallas_call(
        place,
        out_shape=results,
        in_specs=[anywhere] * 5,
        out_specs=(anywhere,) * 5,
        scratch_shapes=[pltpu.VMEM(r.shape, r.dtype) for r in results] + [dma((2, 8))],
        compiler_params=pltpu.CompilerParams(vmem_limit_bytes=64 * 1024 * 1024),
        name="place",
    )(*outs)


def solution(mesh):
    rows, owned = P(("dp", "node"), None), P("node", None)
    return jax.shard_map(
        on_device,
        mesh=mesh,
        in_specs=(rows, rows, rows, owned, owned, owned, owned),
        out_specs=(rows, rows, rows, owned, owned),
        check_vma=False,
    )
```

```python
import math

import jax
import jax.numpy as jnp
from jax import lax
from jax.experimental import pallas as pl
from jax.experimental.pallas import tpu as pltpu
from jax.sharding import PartitionSpec as P

MESH = pl.DeviceIdType.MESH
F32, BF16, I16 = jnp.float32, jnp.bfloat16, jnp.int16
NX, NY, NZ = 4, 8, 12
HALF = NZ // 2
ROWS = 32
KVW = 256
COLS = 2 * KVW
TOK = 256
DH = 1024
REDUCERS = 4
STEPS = 32766.0
TINY = 1e-30


def coordinates():
    dp, node = lax.axis_index("dp"), lax.axis_index("node")
    x = lax.rem(node, NX)
    y = lax.rem(node // NX, NY)
    half = node // (NX * NY)
    low = dp // 2
    core = lax.rem(dp, 2)
    return x, y, half, low, core


def device(x, y, z, core):
    return {
        "dp": lax.rem(z, HALF) * 2 + core,
        "node": (z // HALF) * (NX * NY) + y * NX + x,
    }


def shard_rows(mant, expo_t):
    factor = jnp.zeros(expo_t.shape, F32)
    for exponent in range(-2, 2):
        factor = factor + jnp.where(expo_t == exponent, F32(2.0**exponent), F32(0.0))
    parts = []
    for block in range(2):
        spread = lax.dot_general(
            factor[block : block + 1, :],
            jnp.ones((1, 128), F32),
            (((0,), (0,)), ((), ())),
            preferred_element_type=F32,
        )
        parts.append(mant[:, block * 128 : (block + 1) * 128].astype(F32) * spread)
    return jnp.concatenate(parts, axis=1).astype(BF16)


def over_rows(left, right):
    return lax.dot_general(left, right, (((0,), (0,)), ((), ())), preferred_element_type=F32)


def over_cols(left, right):
    return lax.dot_general(left, right, (((1,), (1,)), ((), ())), preferred_element_type=F32)


def kernel(
    tokens, key_cot, value_cot, key_mant, value_mant, key_expo, value_expo,
    keys, values, tokens_grad, key_grad, value_grad,
    tok, tok2, cot, cot2, mant, expo, part, codes, peaks, codes_in, peaks_in,
    sums, sums_in, total, total_in, final, own_w, other_w, tgrad, kv, kv_out,
    load_sem, store_sem, send_c, recv_c, send_x, recv_x, send_y, recv_y,
    send_z, recv_z, send_g, recv_g, answered, send_wz, recv_wz, send_wy, recv_wy, send_wx, recv_wx,
):
    x, y, half, low, core = coordinates()
    z = half * HALF + low
    sibling = device(x, y, z, 1 - core)
    home = core == half
    mine = pl.multiple_of(core * DH, DH)
    theirs = pl.multiple_of((1 - core) * DH, DH)

    def remote(src, dst, send, recv, to):
        return pltpu.make_async_remote_copy(
            src_ref=src, dst_ref=dst, send_sem=send, recv_sem=recv, device_id=to, device_id_type=MESH
        )

    loads = [
        pltpu.make_async_copy(key_mant, mant.at[0], load_sem.at[0]),
        pltpu.make_async_copy(value_mant, mant.at[1], load_sem.at[1]),
        pltpu.make_async_copy(key_expo, expo.at[0], load_sem.at[2]),
        pltpu.make_async_copy(value_expo, expo.at[1], load_sem.at[3]),
        pltpu.make_async_copy(tokens, tok, load_sem.at[4]),
        pltpu.make_async_copy(key_cot, cot.at[0], load_sem.at[5]),
        pltpu.make_async_copy(value_cot, cot.at[1], load_sem.at[6]),
    ]
    for load in loads:
        load.start()

    barrier = pltpu.get_barrier_semaphore()

    def greet(to):
        pl.semaphore_signal(barrier, inc=1, device_id=to, device_id_type=MESH)

    for d in range(NZ - 1, 0, -1):

        @pl.when(z + d < NZ)
        def _(d=d):
            greet(device(x, y, z + d, core))

    for d in (4, 3, 5, 2, 6, 1, 7):
        greet(device(x, lax.rem(y + d, NY), z, core))
    for d in (2, 1, 3):
        greet(device(lax.rem(x + d, NX), y, z, core))
    greet(sibling)

    for load in loads[:4]:
        load.wait()

    @pl.when(home)
    def _():
        own_w[y, x, :, 0:KVW] = shard_rows(mant[0], expo[0])
        own_w[y, x, :, KVW:COLS] = shard_rows(mant[1], expo[1])

    for load in loads[4:]:
        load.wait()

    def own_part(b, _):
        left = tok[:, pl.ds(pl.multiple_of(b * 128, 128), 128)]
        part[b] = over_rows(left, cot[core]).reshape(NX, ROWS, KVW)
        return 0

    lax.fori_loop(0, 2 * NY, own_part, 0)
    pl.semaphore_wait(barrier, z + (NY - 1) + (NX - 1) + 1)
    for d in range(NZ - 1, 0, -1):

        @pl.when(z >= d)
        def _(d=d):
            pl.semaphore_signal(
                answered, inc=1, device_id=device(x, y, z - d, core), device_id_type=MESH
            )

    def wait_answers():
        @pl.when(z < NZ - 1)
        def _():
            pl.semaphore_wait(answered, NZ - 1 - z)


    swap_cot = remote(cot.at[1 - core], cot2, send_c.at[0], recv_c.at[0], sibling)
    swaps = [
        remote(tok.at[:, pl.ds(h * DH, DH)], tok2.at[h], send_c.at[1 + h], recv_c.at[1 + h], sibling)
        for h in range(2)
    ]
    swap_cot.start()
    for swap in swaps:
        swap.start()

    edge = jnp.logical_or(low == 0, low == HALF - 1)
    outward = 2 * (low // (HALF - 1)) - 1

    def w_z(k):
        to = device(x, y, lax.rem(z + NZ + outward * k, NZ), core)
        return remote(own_w.at[y, x], own_w.at[y, x], send_wz.at[k - 1], recv_wz, to)

    def send_shard(of):
        @pl.when(jnp.logical_and(jnp.logical_and(home, edge), half == of))
        def _():
            for k in (3, 2, 1):
                w_z(k).start()

    send_shard(1)

    def x_copies(h, d):
        to = device(lax.rem(x + d, NX), y, z, core)
        return (
            remote(codes.at[h, d - 1], codes_in.at[h, d - 1],
                   send_x.at[0, h, d - 1], recv_x.at[0, h, d - 1], to),
            remote(peaks.at[h, d - 1], peaks_in.at[h, d - 1],
                   send_x.at[1, h, d - 1], recv_x.at[1, h, d - 1], to),
        )

    swap_cot.wait_recv()
    for h in range(2):
        swaps[h].wait_recv()

        def encode(j, _, h=h):
            left = tok2[h, :, pl.ds(pl.multiple_of(j * 128, 128), 128)]
            b = h * NY + j
            part[b] = part[b] + over_rows(left, cot2[...]).reshape(NX, ROWS, KVW)
            for d in range(1, NX):
                chunk = part[b, lax.rem(x + d, NX)]
                peak = jnp.maximum(jnp.max(jnp.abs(chunk), axis=0, keepdims=True), TINY)
                codes[h, d - 1, j] = jnp.round(chunk * (STEPS / peak)).astype(jnp.int32).astype(I16)
                peaks[h, d - 1, pl.ds(j, 1), :] = peak * (1.0 / STEPS)
            return 0

        lax.fori_loop(0, NY, encode, 0)
        for d in (2, 1, 3):
            for copy in x_copies(h, d):
                copy.start()

    @pl.when(edge)
    def _():
        wait_answers()

    send_shard(0)

    @pl.when(jnp.logical_not(home))
    def _():
        w_z(1).wait_recv()

    def w_y(d, block):
        to = device(x, lax.rem(y + d, NY), z, core)
        return remote(own_w.at[block, x], own_w.at[block, x], send_wy.at[d - 1], recv_wy.at[d - 1], to)

    for d in (4, 3, 5, 2, 6, 1, 7):
        w_y(d, y).start()

    def y_copy(h, d, block):
        to = device(x, lax.rem(y + d, NY), z, core)
        return remote(sums.at[h, block], sums_in.at[h, d - 1], send_y.at[h, d - 1], recv_y.at[h, d - 1], to)

    for h in range(2):
        for d in (2, 1, 3):
            for copy in x_copies(h, d):
                copy.wait_recv()

        def add_x(j, _, h=h):
            value = part[h * NY + j, x]
            for d in range(1, NX):
                scale = peaks_in[h, d - 1, pl.ds(j, 1), :]
                value = value + codes_in[h, d - 1, j].astype(jnp.int32).astype(F32) * scale
            sums[h, j] = value
            return 0

        lax.fori_loop(0, NY, add_x, 0)
        for d in (4, 3, 5, 2, 6, 1, 7):
            y_copy(h, d, lax.rem(y + d, NY)).start()

    for d in range(1, NY):
        w_y(d, lax.rem(y + NY - d, NY)).wait_recv()

    def w_x(d, column):
        to = device(lax.rem(x + d, NX), y, z, core)
        return remote(own_w.at[:, column], own_w.at[:, column], send_wx.at[d - 1], recv_wx.at[d - 1], to)

    for d in (2, 1, 3):
        w_x(d, x).start()

    scale = F32(1.0 / math.sqrt(NX * NY * NZ * 2 * TOK))
    reducing = low < REDUCERS

    def z_copy(h, j, slot):
        to = device(x, y, h * HALF + j, core)
        return remote(total.at[h, j], total_in.at[slot], send_z.at[h, j], recv_z.at[slot], to)

    def rows_of(j):
        return pl.ds(pl.multiple_of(8 * j, 8), 8)

    def g_copy(row, d):
        to = device(x, y, half * HALF + lax.rem(low + d, HALF), core)
        rows = final.at[core, rows_of(row)]
        return remote(rows, rows, send_g.at[d - 1], recv_g.at[row], to)

    def send_sums(h):
        for d in range(1, NY):
            y_copy(h, d, y).wait_recv()
        value = sums[h, y]
        for d in range(1, NY):
            value = value + sums_in[h, d - 1]
        total[h] = value.reshape(REDUCERS, 8, KVW)
        for j in range(REDUCERS):

            @pl.when(z != h * HALF + j)
            def _(j=j):
                z_copy(h, j, z).start()

    def reduce_sums(h):
        @pl.when(jnp.logical_and(half == h, reducing))
        def _():
            for d in range(1, NZ):
                z_copy(h, 0, lax.rem(z + d, NZ)).wait_recv()
            value = total[h, low]
            for d in range(1, NZ):
                value = value + total_in[lax.rem(z + d, NZ)]
            final[core, rows_of(low), :] = value * scale
            for d in (3, 2, 4, 1, 5):
                g_copy(low, d).start()

    @pl.when(jnp.logical_not(edge))
    def _():
        wait_answers()

    send_sums(0)
    reduce_sums(0)
    send_sums(1)

    for d in range(1, NX):
        w_x(d, lax.rem(x + NX - d, NX)).wait_recv()
    w_c = remote(own_w, other_w, send_c.at[3], recv_c.at[3], sibling)
    w_c.start()

    def products(weights, which, columns, store):
        grad = over_cols(cot[0], weights[:, 0:KVW]) + over_cols(cot[1], weights[:, KVW:COLS])
        tgrad[which] = grad.astype(BF16)
        out = pltpu.make_async_copy(tgrad.at[which], tokens_grad.at[:, pl.ds(columns, DH)], store_sem.at[store])
        out.start()
        return out, jnp.dot(tok[:, pl.ds(columns, DH)], weights, preferred_element_type=F32)

    out_mine, kv[...] = products(own_w[...].reshape(DH, COLS), core, mine, 0)
    reduce_sums(1)
    w_c.wait_recv()
    out_theirs, rest = products(other_w[...].reshape(DH, COLS), 1 - core, theirs, 1)
    kv_out[...] = (kv[...] + rest).astype(BF16)
    outs = [
        pltpu.make_async_copy(kv_out.at[:, pl.ds(0, KVW)], keys, store_sem.at[2]),
        pltpu.make_async_copy(kv_out.at[:, pl.ds(KVW, KVW)], values, store_sem.at[3]),
    ]
    for out in outs:
        out.start()

    for j in range(REDUCERS):

        @pl.when(low != j)
        def _(j=j):
            g_copy(j, 1).wait_recv()

    final_c = remote(final.at[core], final.at[core], send_c.at[4], recv_c.at[4], sibling)
    final_c.start()
    remote(final.at[1 - core], final.at[1 - core], send_c.at[4], recv_c.at[4], sibling).wait_recv()
    outs += [
        pltpu.make_async_copy(final.at[0], key_grad, store_sem.at[4]),
        pltpu.make_async_copy(final.at[1], value_grad, store_sem.at[5]),
    ]
    for out in outs[2:]:
        out.start()

    swap_cot.wait_send()
    for swap in swaps:
        swap.wait_send()

    @pl.when(jnp.logical_and(home, edge))
    def _():
        for k in (1, 2, 3):
            w_z(k).wait_send()

    for h in range(2):
        for d in range(1, NX):
            for copy in x_copies(h, d):
                copy.wait_send()
        for d in range(1, NY):
            y_copy(h, d, y).wait_send()
        for j in range(REDUCERS):

            @pl.when(z != h * HALF + j)
            def _(h=h, j=j):
                z_copy(h, j, z).wait_send()

    for d in range(1, NY):
        w_y(d, y).wait_send()
    for d in range(1, NX):
        w_x(d, x).wait_send()
    w_c.wait_send()

    @pl.when(reducing)
    def _():
        for d in range(1, HALF):
            g_copy(low, d).wait_send()

    final_c.wait_send()
    out_mine.wait()
    out_theirs.wait()
    for out in outs:
        out.wait()


def place(*refs):
    sources, outs, staged, sems = refs[:5], refs[5:10], refs[10:15], refs[15]
    pieces = [(2, pl.ds(i * 64, 64)) for i in range(4)]
    pieces += [(i, pl.ds(0, sources[i].shape[0])) for i in (0, 1, 3, 4)]
    loads = [
        pltpu.make_async_copy(sources[i].at[rows], staged[i].at[rows], sems.at[0, k])
        for k, (i, rows) in enumerate(pieces)
    ]
    stores = [
        pltpu.make_async_copy(staged[i].at[rows], outs[i].at[rows], sems.at[1, k])
        for k, (i, rows) in enumerate(pieces)
    ]
    for load in loads:
        load.start()
    for load, store in zip(loads, stores):
        load.wait()
        store.start()
    for store in stores:
        store.wait()


def on_device(tokens, key_cot, value_cot, key_mant, value_mant, key_expo, value_expo):
    dma = pltpu.SemaphoreType.DMA
    shape = jax.ShapeDtypeStruct
    anywhere = pl.BlockSpec(memory_space=pl.ANY)
    results = (
        shape((TOK, KVW), BF16),
        shape((TOK, KVW), BF16),
        shape((TOK, 2 * DH), BF16),
        shape((ROWS, KVW), F32),
        shape((ROWS, KVW), F32),
    )
    outs = pl.pallas_call(
        kernel,
        out_shape=results,
        in_specs=[anywhere] * 7,
        out_specs=(anywhere,) * 5,
        scratch_shapes=[
            pltpu.VMEM((TOK, 2 * DH), BF16),
            pltpu.VMEM((2, TOK, DH), BF16),
            pltpu.VMEM((2, TOK, KVW), BF16),
            pltpu.VMEM((TOK, KVW), BF16),
            pltpu.VMEM((2, ROWS, KVW), BF16),
            pltpu.VMEM((2, 2, ROWS), jnp.int32),
            pltpu.VMEM((2 * NY, NX, ROWS, KVW), F32),
            pltpu.VMEM((2, NX - 1, NY, ROWS, KVW), I16),
            pltpu.VMEM((2, NX - 1, NY, KVW), F32),
            pltpu.VMEM((2, NX - 1, NY, ROWS, KVW), I16),
            pltpu.VMEM((2, NX - 1, NY, KVW), F32),
            pltpu.VMEM((2, NY, ROWS, KVW), F32),
            pltpu.VMEM((2, NY - 1, ROWS, KVW), F32),
            pltpu.VMEM((2, REDUCERS, 8, KVW), F32),
            pltpu.VMEM((NZ, 8, KVW), F32),
            pltpu.VMEM((2, ROWS, KVW), F32),
            pltpu.VMEM((NY, NX, ROWS, COLS), BF16),
            pltpu.VMEM((NY, NX, ROWS, COLS), BF16),
            pltpu.VMEM((2, TOK, DH), BF16),
            pltpu.VMEM((TOK, COLS), F32),
            pltpu.VMEM((TOK, COLS), BF16),
            dma((7,)),
            dma((6,)),
            dma((5,)), dma((5,)),
            dma((2, 2, NX - 1)), dma((2, 2, NX - 1)),
            dma((2, NY - 1)), dma((2, NY - 1)),
            dma((2, REDUCERS)), dma((NZ,)),
            dma((HALF - 1,)), dma((REDUCERS,)),
            pltpu.SemaphoreType.REGULAR,
            dma((3,)), dma,
            dma((NY - 1,)), dma((NY - 1,)),
            dma((NX - 1,)), dma((NX - 1,)),
        ],
        compiler_params=pltpu.CompilerParams(
            collective_id=0, has_side_effects=True, vmem_limit_bytes=64 * 1024 * 1024
        ),
        name="projections",
    )(tokens, key_cot, value_cot, key_mant, value_mant, key_expo.T, value_expo.T)
    return pl.pallas_call(
        place,
        out_shape=results,
        in_specs=[anywhere] * 5,
        out_specs=(anywhere,) * 5,
        scratch_shapes=[pltpu.VMEM(r.shape, r.dtype) for r in results] + [dma((2, 8))],
        compiler_params=pltpu.CompilerParams(vmem_limit_bytes=64 * 1024 * 1024),
        name="place",
    )(*outs)


def solution(mesh):
    rows, owned = P(("dp", "node"), None), P("node", None)
    return jax.shard_map(
        on_device,
        mesh=mesh,
        in_specs=(rows, rows, rows, owned, owned, owned, owned),
        out_specs=(rows, rows, rows, owned, owned),
        check_vma=False,
    )
```

```python
import math

import jax
import jax.numpy as jnp
from jax import lax
from jax.experimental import pallas as pl
from jax.experimental.pallas import tpu as pltpu
from jax.sharding import PartitionSpec as P

MESH = pl.DeviceIdType.MESH
F32, BF16, I16 = jnp.float32, jnp.bfloat16, jnp.int16
NX, NY, NZ = 4, 8, 12
HALF = NZ // 2
ROWS = 32
KVW = 256
COLS = 2 * KVW
TOK = 256
DH = 1024
REDUCERS = 4
STEPS = 32766.0
TINY = 1e-30


def coordinates():
    dp, node = lax.axis_index("dp"), lax.axis_index("node")
    x = lax.rem(node, NX)
    y = lax.rem(node // NX, NY)
    half = node // (NX * NY)
    low = dp // 2
    core = lax.rem(dp, 2)
    return x, y, half, low, core


def device(x, y, z, core):
    return {
        "dp": lax.rem(z, HALF) * 2 + core,
        "node": (z // HALF) * (NX * NY) + y * NX + x,
    }


def shard_rows(mant, expo_t):
    factor = jnp.zeros(expo_t.shape, F32)
    for exponent in range(-2, 2):
        factor = factor + jnp.where(expo_t == exponent, F32(2.0**exponent), F32(0.0))
    parts = []
    for block in range(2):
        spread = lax.dot_general(
            factor[block : block + 1, :],
            jnp.ones((1, 128), F32),
            (((0,), (0,)), ((), ())),
            preferred_element_type=F32,
        )
        parts.append(mant[:, block * 128 : (block + 1) * 128].astype(F32) * spread)
    return jnp.concatenate(parts, axis=1).astype(BF16)


def over_rows(left, right):
    return lax.dot_general(left, right, (((0,), (0,)), ((), ())), preferred_element_type=F32)


def over_cols(left, right):
    return lax.dot_general(left, right, (((1,), (1,)), ((), ())), preferred_element_type=F32)


def kernel(
    tokens, key_cot, value_cot, key_mant, value_mant, key_expo, value_expo,
    keys, values, tokens_grad, key_grad, value_grad,
    tok, tok2, cot, cot2, mant, expo, part, codes, peaks, codes_in, peaks_in,
    sums, codes_y, peaks_y, codes_y_in, peaks_y_in, total, total_in, final, own_w, other_w, tgrad, kv, kv_out,
    load_sem, store_sem, send_c, recv_c, send_x, recv_x, send_y, recv_y,
    send_z, recv_z, send_g, recv_g, answered, send_wz, recv_wz, send_wy, recv_wy, send_wx, recv_wx,
):
    x, y, half, low, core = coordinates()
    z = half * HALF + low
    sibling = device(x, y, z, 1 - core)
    home = core == half
    mine = pl.multiple_of(core * DH, DH)
    theirs = pl.multiple_of((1 - core) * DH, DH)

    def remote(src, dst, send, recv, to):
        return pltpu.make_async_remote_copy(
            src_ref=src, dst_ref=dst, send_sem=send, recv_sem=recv, device_id=to, device_id_type=MESH
        )

    loads = [
        pltpu.make_async_copy(key_mant, mant.at[0], load_sem.at[0]),
        pltpu.make_async_copy(value_mant, mant.at[1], load_sem.at[1]),
        pltpu.make_async_copy(key_expo, expo.at[0], load_sem.at[2]),
        pltpu.make_async_copy(value_expo, expo.at[1], load_sem.at[3]),
        pltpu.make_async_copy(tokens, tok, load_sem.at[4]),
        pltpu.make_async_copy(key_cot, cot.at[0], load_sem.at[5]),
        pltpu.make_async_copy(value_cot, cot.at[1], load_sem.at[6]),
    ]
    for load in loads:
        load.start()

    barrier = pltpu.get_barrier_semaphore()

    def greet(to):
        pl.semaphore_signal(barrier, inc=1, device_id=to, device_id_type=MESH)

    for d in range(NZ - 1, 0, -1):

        @pl.when(z + d < NZ)
        def _(d=d):
            greet(device(x, y, z + d, core))

    for d in (4, 3, 5, 2, 6, 1, 7):
        greet(device(x, lax.rem(y + d, NY), z, core))
    for d in (2, 1, 3):
        greet(device(lax.rem(x + d, NX), y, z, core))
    greet(sibling)

    for load in loads[:4]:
        load.wait()

    @pl.when(home)
    def _():
        own_w[y, x, :, 0:KVW] = shard_rows(mant[0], expo[0])
        own_w[y, x, :, KVW:COLS] = shard_rows(mant[1], expo[1])

    for load in loads[4:]:
        load.wait()

    def own_part(b):
        left = tok[:, pl.ds(pl.multiple_of(b * 128, 128), 128)]
        return over_rows(left, cot[core]).reshape(NX, ROWS, KVW)

    def first_part(b, _):
        part[b] = own_part(b)
        return 0

    lax.fori_loop(0, NY, first_part, 0)
    pl.semaphore_wait(barrier, z + (NY - 1) + (NX - 1) + 1)
    for d in range(NZ - 1, 0, -1):

        @pl.when(z >= d)
        def _(d=d):
            pl.semaphore_signal(
                answered, inc=1, device_id=device(x, y, z - d, core), device_id_type=MESH
            )

    def wait_answers():
        @pl.when(z < NZ - 1)
        def _():
            pl.semaphore_wait(answered, NZ - 1 - z)


    swap_cot = remote(cot.at[1 - core], cot2, send_c.at[0], recv_c.at[0], sibling)
    swaps = [
        remote(tok.at[:, pl.ds(h * DH, DH)], tok2.at[h], send_c.at[1 + h], recv_c.at[1 + h], sibling)
        for h in range(2)
    ]
    swap_cot.start()
    swaps[0].start()

    edge = jnp.logical_or(low == 0, low == HALF - 1)
    outward = 2 * (low // (HALF - 1)) - 1

    def w_z(k):
        to = device(x, y, lax.rem(z + NZ + outward * k, NZ), core)
        return remote(own_w.at[y, x], own_w.at[y, x], send_wz.at[k - 1], recv_wz, to)

    def send_shard(of):
        @pl.when(jnp.logical_and(jnp.logical_and(home, edge), half == of))
        def _():
            for k in (3, 2, 1):
                w_z(k).start()

    send_shard(1)

    def x_copies(h, d):
        to = device(lax.rem(x + d, NX), y, z, core)
        return (
            remote(codes.at[h, d - 1], codes_in.at[h, d - 1],
                   send_x.at[0, h, d - 1], recv_x.at[0, h, d - 1], to),
            remote(peaks.at[h, d - 1], peaks_in.at[h, d - 1],
                   send_x.at[1, h, d - 1], recv_x.at[1, h, d - 1], to),
        )

    def coded(chunk):
        peak = jnp.maximum(jnp.max(jnp.abs(chunk), axis=0, keepdims=True), TINY)
        codes_of = jnp.round(chunk * (STEPS / peak)).astype(jnp.int32).astype(I16)
        return codes_of, peak * (1.0 / STEPS)

    def decoded(codes_of, scales):
        return codes_of.astype(jnp.int32).astype(F32) * scales

    swap_cot.wait_recv()
    for h in range(2):
        swaps[h].wait_recv()
        if h == 0:
            swaps[1].start()

        def both_parts(j, _, h=h):
            left = tok2[h, :, pl.ds(pl.multiple_of(j * 128, 128), 128)]
            b = h * NY + j
            first = part[b] if h == 0 else own_part(b)
            part[b] = first + over_rows(left, cot2[...]).reshape(NX, ROWS, KVW)
            return 0

        lax.fori_loop(0, NY, both_parts, 0)
        for d in (2, 1, 3):

            def encode(j, _, h=h, d=d):
                codes[h, d - 1, j], scales = coded(part[h * NY + j, lax.rem(x + d, NX)])
                peaks[h, d - 1, pl.ds(j, 1), :] = scales
                return 0

            lax.fori_loop(0, NY, encode, 0)
            if h == 0:
                for copy in x_copies(0, d):
                    copy.start()

    @pl.when(edge)
    def _():
        wait_answers()

    send_shard(0)

    @pl.when(jnp.logical_not(home))
    def _():
        w_z(1).wait_recv()

    def w_y(d, block):
        to = device(x, lax.rem(y + d, NY), z, core)
        return remote(own_w.at[block, x], own_w.at[block, x], send_wy.at[d - 1], recv_wy.at[d - 1], to)

    for d in (4, 3, 5, 2, 6, 1, 7):
        w_y(d, y).start()

    for d in (2, 1, 3):
        for copy in x_copies(0, d):
            copy.wait_send()
    for d in (2, 1, 3):
        for copy in x_copies(1, d):
            copy.start()

    def y_copies(h, d, block):
        to = device(x, lax.rem(y + d, NY), z, core)
        return (
            remote(codes_y.at[h, block], codes_y_in.at[h, d - 1],
                   send_y.at[0, h, d - 1], recv_y.at[0, h, d - 1], to),
            remote(peaks_y.at[h, block], peaks_y_in.at[h, d - 1],
                   send_y.at[1, h, d - 1], recv_y.at[1, h, d - 1], to),
        )

    def sum_x(h):
        for d in (2, 1, 3):
            for copy in x_copies(h, d):
                copy.wait_recv()

        def add_x(block):
            value = part[h * NY + block, x]
            for d in range(1, NX):
                value = value + decoded(codes_in[h, d - 1, block], peaks_in[h, d - 1, pl.ds(block, 1), :])
            return value

        def add_and_send(i, _):
            d = NY // 2 + (1 - 2 * lax.rem(i, 2)) * ((i + 1) // 2)
            block = lax.rem(y + d, NY)
            codes_y[h, block], peaks_y[h, block] = coded(add_x(block))
            for copy in y_copies(h, d, block):
                copy.start()
            return 0

        lax.fori_loop(0, NY - 1, add_and_send, 0)
        sums[h] = add_x(y)

    sum_x(0)

    for d in (2, 1, 3):
        for copy in x_copies(1, d):
            copy.wait_send()
    for d in range(1, NY):
        w_y(d, lax.rem(y + NY - d, NY)).wait_recv()

    def w_x(d, column):
        to = device(lax.rem(x + d, NX), y, z, core)
        return remote(own_w.at[:, column], own_w.at[:, column], send_wx.at[d - 1], recv_wx.at[d - 1], to)

    for d in (2, 1, 3):
        w_x(d, x).start()

    scale = F32(1.0 / math.sqrt(NX * NY * NZ * 2 * TOK))
    reducing = low < REDUCERS

    def z_copy(h, j, slot):
        to = device(x, y, h * HALF + j, core)
        return remote(total.at[h, j], total_in.at[slot], send_z.at[h, j], recv_z.at[slot], to)

    def rows_of(j):
        return pl.ds(pl.multiple_of(8 * j, 8), 8)

    def g_copy(row, d):
        to = device(x, y, half * HALF + lax.rem(low + d, HALF), core)
        rows = final.at[core, rows_of(row)]
        return remote(rows, rows, send_g.at[d - 1], recv_g.at[row], to)

    def send_sums(h):
        for d in range(1, NY):
            for copy in y_copies(h, d, y):
                copy.wait_recv()
        value = sums[h]
        for d in range(1, NY):
            value = value + decoded(codes_y_in[h, d - 1], peaks_y_in[h, d - 1])
        total[h] = value.reshape(REDUCERS, 8, KVW)
        for j in range(REDUCERS):

            @pl.when(z != h * HALF + j)
            def _(j=j):
                z_copy(h, j, z).start()

    def reduce_sums(h):
        @pl.when(jnp.logical_and(half == h, reducing))
        def _():
            for d in range(1, NZ):
                z_copy(h, 0, lax.rem(z + d, NZ)).wait_recv()
            value = total[h, low]
            for d in range(1, NZ):
                value = value + total_in[lax.rem(z + d, NZ)]
            final[core, rows_of(low), :] = value * scale
            for d in (3, 2, 4, 1, 5):
                g_copy(low, d).start()

    @pl.when(jnp.logical_not(edge))
    def _():
        wait_answers()

    send_sums(0)
    sum_x(1)
    send_sums(1)
    reduce_sums(0)

    for d in range(1, NX):
        w_x(d, lax.rem(x + NX - d, NX)).wait_recv()
    w_c = remote(own_w, other_w, send_c.at[3], recv_c.at[3], sibling)
    w_c.start()

    def products(weights, which, columns, store):
        grad = over_cols(cot[0], weights[:, 0:KVW]) + over_cols(cot[1], weights[:, KVW:COLS])
        tgrad[which] = grad.astype(BF16)
        out = pltpu.make_async_copy(tgrad.at[which], tokens_grad.at[:, pl.ds(columns, DH)], store_sem.at[store])
        out.start()
        return out, jnp.dot(tok[:, pl.ds(columns, DH)], weights, preferred_element_type=F32)

    out_mine, kv[...] = products(own_w[...].reshape(DH, COLS), core, mine, 0)
    reduce_sums(1)
    w_c.wait_recv()
    out_theirs, rest = products(other_w[...].reshape(DH, COLS), 1 - core, theirs, 1)
    kv_out[...] = (kv[...] + rest).astype(BF16)
    outs = [
        pltpu.make_async_copy(kv_out.at[:, pl.ds(0, KVW)], keys, store_sem.at[2]),
        pltpu.make_async_copy(kv_out.at[:, pl.ds(KVW, KVW)], values, store_sem.at[3]),
    ]
    for out in outs:
        out.start()

    for j in range(REDUCERS):

        @pl.when(low != j)
        def _(j=j):
            g_copy(j, 1).wait_recv()

    final_c = remote(final.at[core], final.at[core], send_c.at[4], recv_c.at[4], sibling)
    final_c.start()
    remote(final.at[1 - core], final.at[1 - core], send_c.at[4], recv_c.at[4], sibling).wait_recv()
    outs += [
        pltpu.make_async_copy(final.at[0], key_grad, store_sem.at[4]),
        pltpu.make_async_copy(final.at[1], value_grad, store_sem.at[5]),
    ]
    for out in outs[2:]:
        out.start()

    swap_cot.wait_send()
    for swap in swaps:
        swap.wait_send()

    @pl.when(jnp.logical_and(home, edge))
    def _():
        for k in (1, 2, 3):
            w_z(k).wait_send()

    for h in range(2):
        for d in range(1, NY):
            for copy in y_copies(h, d, y):
                copy.wait_send()
        for j in range(REDUCERS):

            @pl.when(z != h * HALF + j)
            def _(h=h, j=j):
                z_copy(h, j, z).wait_send()

    for d in range(1, NY):
        w_y(d, y).wait_send()
    for d in range(1, NX):
        w_x(d, x).wait_send()
    w_c.wait_send()

    @pl.when(reducing)
    def _():
        for d in range(1, HALF):
            g_copy(low, d).wait_send()

    final_c.wait_send()
    out_mine.wait()
    out_theirs.wait()
    for out in outs:
        out.wait()


def place(*refs):
    sources, outs, staged, sems = refs[:5], refs[5:10], refs[10:15], refs[15]
    pieces = [(2, pl.ds(i * 64, 64)) for i in range(4)]
    pieces += [(i, pl.ds(0, sources[i].shape[0])) for i in (0, 1, 3, 4)]
    loads = [
        pltpu.make_async_copy(sources[i].at[rows], staged[i].at[rows], sems.at[0, k])
        for k, (i, rows) in enumerate(pieces)
    ]
    stores = [
        pltpu.make_async_copy(staged[i].at[rows], outs[i].at[rows], sems.at[1, k])
        for k, (i, rows) in enumerate(pieces)
    ]
    for load in loads:
        load.start()
    for load, store in zip(loads, stores):
        load.wait()
        store.start()
    for store in stores:
        store.wait()


def on_device(tokens, key_cot, value_cot, key_mant, value_mant, key_expo, value_expo):
    dma = pltpu.SemaphoreType.DMA
    shape = jax.ShapeDtypeStruct
    anywhere = pl.BlockSpec(memory_space=pl.ANY)
    results = (
        shape((TOK, KVW), BF16),
        shape((TOK, KVW), BF16),
        shape((TOK, 2 * DH), BF16),
        shape((ROWS, KVW), F32),
        shape((ROWS, KVW), F32),
    )
    outs = pl.pallas_call(
        kernel,
        out_shape=results,
        in_specs=[anywhere] * 7,
        out_specs=(anywhere,) * 5,
        scratch_shapes=[
            pltpu.VMEM((TOK, 2 * DH), BF16),
            pltpu.VMEM((2, TOK, DH), BF16),
            pltpu.VMEM((2, TOK, KVW), BF16),
            pltpu.VMEM((TOK, KVW), BF16),
            pltpu.VMEM((2, ROWS, KVW), BF16),
            pltpu.VMEM((2, 2, ROWS), jnp.int32),
            pltpu.VMEM((2 * NY, NX, ROWS, KVW), F32),
            pltpu.VMEM((2, NX - 1, NY, ROWS, KVW), I16),
            pltpu.VMEM((2, NX - 1, NY, KVW), F32),
            pltpu.VMEM((2, NX - 1, NY, ROWS, KVW), I16),
            pltpu.VMEM((2, NX - 1, NY, KVW), F32),
            pltpu.VMEM((2, ROWS, KVW), F32),
            pltpu.VMEM((2, NY, ROWS, KVW), I16),
            pltpu.VMEM((2, NY, 1, KVW), F32),
            pltpu.VMEM((2, NY - 1, ROWS, KVW), I16),
            pltpu.VMEM((2, NY - 1, 1, KVW), F32),
            pltpu.VMEM((2, REDUCERS, 8, KVW), F32),
            pltpu.VMEM((NZ, 8, KVW), F32),
            pltpu.VMEM((2, ROWS, KVW), F32),
            pltpu.VMEM((NY, NX, ROWS, COLS), BF16),
            pltpu.VMEM((NY, NX, ROWS, COLS), BF16),
            pltpu.VMEM((2, TOK, DH), BF16),
            pltpu.VMEM((TOK, COLS), F32),
            pltpu.VMEM((TOK, COLS), BF16),
            dma((7,)),
            dma((6,)),
            dma((5,)), dma((5,)),
            dma((2, 2, NX - 1)), dma((2, 2, NX - 1)),
            dma((2, 2, NY - 1)), dma((2, 2, NY - 1)),
            dma((2, REDUCERS)), dma((NZ,)),
            dma((HALF - 1,)), dma((REDUCERS,)),
            pltpu.SemaphoreType.REGULAR,
            dma((3,)), dma,
            dma((NY - 1,)), dma((NY - 1,)),
            dma((NX - 1,)), dma((NX - 1,)),
        ],
        compiler_params=pltpu.CompilerParams(
            collective_id=0, has_side_effects=True, vmem_limit_bytes=64 * 1024 * 1024
        ),
        name="projections",
    )(tokens, key_cot, value_cot, key_mant, value_mant, key_expo.T, value_expo.T)
    return pl.pallas_call(
        place,
        out_shape=results,
        in_specs=[anywhere] * 5,
        out_specs=(anywhere,) * 5,
        scratch_shapes=[pltpu.VMEM(r.shape, r.dtype) for r in results] + [dma((2, 8))],
        compiler_params=pltpu.CompilerParams(vmem_limit_bytes=64 * 1024 * 1024),
        name="place",
    )(*outs)


def solution(mesh):
    rows, owned = P(("dp", "node"), None), P("node", None)
    return jax.shard_map(
        on_device,
        mesh=mesh,
        in_specs=(rows, rows, rows, owned, owned, owned, owned),
        out_specs=(rows, rows, rows, owned, owned),
        check_vma=False,
    )
```

```python
import math

import jax
import jax.numpy as jnp
from jax import lax
from jax.experimental import pallas as pl
from jax.experimental.pallas import tpu as pltpu
from jax.sharding import PartitionSpec as P

MESH = pl.DeviceIdType.MESH
F32, BF16, I16 = jnp.float32, jnp.bfloat16, jnp.int16
NX, NY, NZ = 4, 8, 12
HALF = NZ // 2
ROWS = 32
KVW = 256
COLS = 2 * KVW
TOK = 256
DH = 1024
REDUCERS = 4
STEPS = 32766.0
TINY = 1e-30


def coordinates():
    dp, node = lax.axis_index("dp"), lax.axis_index("node")
    x = lax.rem(node, NX)
    y = lax.rem(node // NX, NY)
    half = node // (NX * NY)
    low = dp // 2
    core = lax.rem(dp, 2)
    return x, y, half, low, core


def device(x, y, z, core):
    return {
        "dp": lax.rem(z, HALF) * 2 + core,
        "node": (z // HALF) * (NX * NY) + y * NX + x,
    }


def shard_rows(mant, expo_t):
    factor = jnp.zeros(expo_t.shape, F32)
    for exponent in range(-2, 2):
        factor = factor + jnp.where(expo_t == exponent, F32(2.0**exponent), F32(0.0))
    parts = []
    for block in range(2):
        spread = lax.dot_general(
            factor[block : block + 1, :],
            jnp.ones((1, 128), F32),
            (((0,), (0,)), ((), ())),
            preferred_element_type=F32,
        )
        parts.append(mant[:, block * 128 : (block + 1) * 128].astype(F32) * spread)
    return jnp.concatenate(parts, axis=1).astype(BF16)


def over_rows(left, right):
    return lax.dot_general(left, right, (((0,), (0,)), ((), ())), preferred_element_type=F32)


def over_cols(left, right):
    return lax.dot_general(left, right, (((1,), (1,)), ((), ())), preferred_element_type=F32)


def each(count, step):
    def body(i, _):
        step(i)
        return 0

    lax.fori_loop(0, count, body, 0)


def around(i, ring):
    return ring // 2 + (1 - 2 * lax.rem(i, 2)) * ((i + 1) // 2)


def kernel(
    tokens, key_cot, value_cot, key_mant, value_mant, key_expo, value_expo,
    keys, values, tokens_grad, key_grad, value_grad,
    tok, tok2, cot, cot2, mant, expo, part, codes, peaks, codes_in, peaks_in,
    sums, codes_y, peaks_y, codes_y_in, peaks_y_in, total, total_in, final, own_w, other_w, tgrad, kv, kv_out,
    load_sem, store_sem, send_c, recv_c, send_x, recv_x, send_y, recv_y,
    send_z, recv_z, send_g, recv_g, answered, send_wz, recv_wz, send_wy, recv_wy, send_wx, recv_wx,
):
    x, y, half, low, core = coordinates()
    z = half * HALF + low
    sibling = device(x, y, z, 1 - core)
    home = core == half

    def remote(src, dst, send, recv, to):
        return pltpu.make_async_remote_copy(
            src_ref=src, dst_ref=dst, send_sem=send, recv_sem=recv, device_id=to, device_id_type=MESH
        )

    loads = [
        pltpu.make_async_copy(key_mant, mant.at[0], load_sem.at[0]),
        pltpu.make_async_copy(value_mant, mant.at[1], load_sem.at[1]),
        pltpu.make_async_copy(key_expo, expo.at[0], load_sem.at[2]),
        pltpu.make_async_copy(value_expo, expo.at[1], load_sem.at[3]),
        pltpu.make_async_copy(tokens, tok, load_sem.at[4]),
        pltpu.make_async_copy(key_cot, cot.at[0], load_sem.at[5]),
        pltpu.make_async_copy(value_cot, cot.at[1], load_sem.at[6]),
    ]
    for load in loads[4:] + loads[:4]:
        load.start()

    barrier = pltpu.get_barrier_semaphore()

    def greet(to):
        pl.semaphore_signal(barrier, inc=1, device_id=to, device_id_type=MESH)

    each(NY - 1, lambda i: greet(device(x, lax.rem(y + around(i, NY), NY), z, core)))
    each(NX - 1, lambda i: greet(device(lax.rem(x + around(i, NX), NX), y, z, core)))
    greet(sibling)
    each(NZ - 1 - z, lambda i: greet(device(x, y, NZ - 1 - i, core)))

    for load in loads[4:]:
        load.wait()

    def own_part(b):
        left = tok[:, pl.ds(pl.multiple_of(b * 128, 128), 128)]
        return over_rows(left, cot[core]).reshape(NX, ROWS, KVW)

    def first_part(b, _):
        part[b] = own_part(b)
        return 0

    lax.fori_loop(0, NY, first_part, 0)
    pl.semaphore_wait(barrier, z + (NY - 1) + (NX - 1) + 1)
    each(
        z,
        lambda i: pl.semaphore_signal(
            answered, inc=1, device_id=device(x, y, i, core), device_id_type=MESH
        ),
    )

    def wait_answers():
        @pl.when(z < NZ - 1)
        def _():
            pl.semaphore_wait(answered, NZ - 1 - z)


    swap_cot = remote(cot.at[1 - core], cot2, send_c.at[0], recv_c.at[0], sibling)
    swaps = [
        remote(tok.at[:, pl.ds(h * DH, DH)], tok2.at[h], send_c.at[1 + h], recv_c.at[1 + h], sibling)
        for h in range(2)
    ]
    swap_cot.start()
    swaps[0].start()

    for load in loads[:4]:
        load.wait()

    @pl.when(home)
    def _():
        own_w[y, x, :, 0:KVW] = shard_rows(mant[0], expo[0])
        own_w[y, x, :, KVW:COLS] = shard_rows(mant[1], expo[1])

    edge = jnp.logical_or(low == 0, low == HALF - 1)
    outward = 2 * (low // (HALF - 1)) - 1

    def w_z(k):
        to = device(x, y, lax.rem(z + NZ + outward * k, NZ), core)
        return remote(own_w.at[y, x], own_w.at[y, x], send_wz.at[k - 1], recv_wz, to)

    def send_shard(of):
        @pl.when(jnp.logical_and(jnp.logical_and(home, edge), half == of))
        def _():
            each(HALF // 2, lambda i: w_z(HALF // 2 - i).start())

    send_shard(1)

    def x_copies(h, d):
        to = device(lax.rem(x + d, NX), y, z, core)
        return (
            remote(codes.at[h, d - 1], codes_in.at[h, d - 1],
                   send_x.at[0, h, d - 1], recv_x.at[0, h, d - 1], to),
            remote(peaks.at[h, d - 1], peaks_in.at[h, d - 1],
                   send_x.at[1, h, d - 1], recv_x.at[1, h, d - 1], to),
        )

    def coded(chunk):
        peak = jnp.maximum(jnp.max(jnp.abs(chunk), axis=0, keepdims=True), TINY)
        codes_of = jnp.round(chunk * (STEPS / peak)).astype(jnp.int32).astype(I16)
        return codes_of, peak * (1.0 / STEPS)

    def decoded(codes_of, scales):
        return codes_of.astype(jnp.int32).astype(F32) * scales

    swap_cot.wait_recv()
    for h in range(2):
        swaps[h].wait_recv()
        if h == 0:
            swaps[1].start()

        def both_parts(j, _, h=h):
            left = tok2[h, :, pl.ds(pl.multiple_of(j * 128, 128), 128)]
            b = h * NY + j
            first = part[b] if h == 0 else own_part(b)
            part[b] = first + over_rows(left, cot2[...]).reshape(NX, ROWS, KVW)
            return 0

        lax.fori_loop(0, NY, both_parts, 0)
        def encode_for(i, h=h):
            d = around(i, NX)

            def encode(j):
                codes[h, d - 1, j], scales = coded(part[h * NY + j, lax.rem(x + d, NX)])
                peaks[h, d - 1, pl.ds(j, 1), :] = scales

            each(NY, encode)
            if h == 0:
                for copy in x_copies(0, d):
                    copy.start()

        each(NX - 1, encode_for)

    @pl.when(edge)
    def _():
        wait_answers()

    send_shard(0)

    @pl.when(jnp.logical_not(home))
    def _():
        w_z(1).wait_recv()

    def w_y(d, block):
        to = device(x, lax.rem(y + d, NY), z, core)
        return remote(own_w.at[block, x], own_w.at[block, x], send_wy.at[d - 1], recv_wy.at[d - 1], to)

    each(NY - 1, lambda i: w_y(around(i, NY), y).start())

    def wait_sent_x(i, h):
        for copy in x_copies(h, i + 1):
            copy.wait_send()

    def start_x(i):
        for copy in x_copies(1, around(i, NX)):
            copy.start()

    each(NX - 1, lambda i: wait_sent_x(i, 0))
    each(NX - 1, start_x)

    def y_copies(h, d, block):
        to = device(x, lax.rem(y + d, NY), z, core)
        return (
            remote(codes_y.at[h, block], codes_y_in.at[h, d - 1],
                   send_y.at[0, h, d - 1], recv_y.at[0, h, d - 1], to),
            remote(peaks_y.at[h, block], peaks_y_in.at[h, d - 1],
                   send_y.at[1, h, d - 1], recv_y.at[1, h, d - 1], to),
        )

    def sum_x(h):
        def wait_x(i):
            for copy in x_copies(h, i + 1):
                copy.wait_recv()

        each(NX - 1, wait_x)

        def add_x(block):
            value = part[h * NY + block, x]
            for d in range(1, NX):
                value = value + decoded(codes_in[h, d - 1, block], peaks_in[h, d - 1, pl.ds(block, 1), :])
            return value

        def add_and_send(i):
            d = around(i, NY)
            block = lax.rem(y + d, NY)
            codes_y[h, block], peaks_y[h, block] = coded(add_x(block))
            for copy in y_copies(h, d, block):
                copy.start()

        each(NY - 1, add_and_send)
        sums[h] = add_x(y)

    sum_x(0)

    each(NX - 1, lambda i: wait_sent_x(i, 1))
    each(NY - 1, lambda i: w_y(i + 1, lax.rem(y + NY - 1 - i, NY)).wait_recv())

    def w_x(d, column):
        to = device(lax.rem(x + d, NX), y, z, core)
        return remote(own_w.at[:, column], own_w.at[:, column], send_wx.at[d - 1], recv_wx.at[d - 1], to)

    each(NX - 1, lambda i: w_x(around(i, NX), x).start())

    scale = F32(1.0 / math.sqrt(NX * NY * NZ * 2 * TOK))
    reducing = low < REDUCERS

    def z_copy(h, j, slot):
        to = device(x, y, h * HALF + j, core)
        return remote(total.at[h, j], total_in.at[slot], send_z.at[h, j], recv_z.at[slot], to)

    def rows_of(j):
        return pl.ds(pl.multiple_of(8 * j, 8), 8)

    def g_copy(row, d):
        to = device(x, y, half * HALF + lax.rem(low + d, HALF), core)
        rows = final.at[core, rows_of(row)]
        return remote(rows, rows, send_g.at[d - 1], recv_g.at[row], to)

    def send_sums(h):
        def wait_y(i):
            for copy in y_copies(h, i + 1, y):
                copy.wait_recv()

        each(NY - 1, wait_y)
        value = sums[h]
        for d in range(1, NY):
            value = value + decoded(codes_y_in[h, d - 1], peaks_y_in[h, d - 1])
        total[h] = value.reshape(REDUCERS, 8, KVW)

        def send(j):
            @pl.when(z != h * HALF + j)
            def _():
                z_copy(h, j, z).start()

        each(REDUCERS, send)

    def reduce_sums(h):
        @pl.when(jnp.logical_and(half == h, reducing))
        def _():
            each(NZ - 1, lambda i: z_copy(h, 0, lax.rem(z + i + 1, NZ)).wait_recv())
            value = total[h, low]
            for d in range(1, NZ):
                value = value + total_in[lax.rem(z + d, NZ)]
            final[core, rows_of(low), :] = value * scale
            each(HALF - 1, lambda i: g_copy(low, around(i, HALF)).start())

    @pl.when(jnp.logical_not(edge))
    def _():
        wait_answers()

    send_sums(0)
    sum_x(1)
    send_sums(1)
    reduce_sums(0)

    each(NX - 1, lambda i: w_x(i + 1, lax.rem(x + NX - 1 - i, NX)).wait_recv())
    w_c = remote(own_w, other_w, send_c.at[3], recv_c.at[3], sibling)
    w_c.start()

    def products(weights, which, first):
        def tile(t):
            rows = weights[pl.ds(t * 2, 2)].reshape(256, COLS)
            at = pl.ds(pl.multiple_of(t * 256, 256), 256)
            grad = over_cols(cot[0], rows[:, 0:KVW]) + over_cols(cot[1], rows[:, KVW:COLS])
            tgrad[which, :, at] = grad.astype(BF16)
            left = tok[:, pl.ds(pl.multiple_of(which * DH + t * 256, 256), 256)]
            kv[...] = kv[...] + jnp.dot(left, rows, preferred_element_type=F32)

        if first:
            kv[...] = jnp.zeros_like(kv)
        each(NY // 2, tile)
        columns = pl.ds(pl.multiple_of(which * DH, DH), DH)
        out = pltpu.make_async_copy(tgrad.at[which], tokens_grad.at[:, columns], store_sem.at[0 if first else 1])
        out.start()
        return out

    out_mine = products(own_w, core, True)
    reduce_sums(1)
    w_c.wait_recv()
    out_theirs = products(other_w, 1 - core, False)
    kv_out[...] = kv[...].astype(BF16)
    outs = [
        pltpu.make_async_copy(kv_out.at[:, pl.ds(0, KVW)], keys, store_sem.at[2]),
        pltpu.make_async_copy(kv_out.at[:, pl.ds(KVW, KVW)], values, store_sem.at[3]),
    ]
    for out in outs:
        out.start()

    def wait_rows(j):
        @pl.when(low != j)
        def _():
            g_copy(j, 1).wait_recv()

    each(REDUCERS, wait_rows)

    final_c = remote(final.at[core], final.at[core], send_c.at[4], recv_c.at[4], sibling)
    final_c.start()
    remote(final.at[1 - core], final.at[1 - core], send_c.at[4], recv_c.at[4], sibling).wait_recv()
    outs += [
        pltpu.make_async_copy(final.at[0], key_grad, store_sem.at[4]),
        pltpu.make_async_copy(final.at[1], value_grad, store_sem.at[5]),
    ]
    for out in outs[2:]:
        out.start()

    swap_cot.wait_send()
    for swap in swaps:
        swap.wait_send()

    @pl.when(jnp.logical_and(home, edge))
    def _():
        each(HALF // 2, lambda i: w_z(i + 1).wait_send())

    def sent_y(i):
        for h in range(2):
            for copy in y_copies(h, i + 1, y):
                copy.wait_send()
        w_y(i + 1, y).wait_send()

    def sent_z(j):
        for h in range(2):

            @pl.when(z != h * HALF + j)
            def _(h=h):
                z_copy(h, j, z).wait_send()

    each(NY - 1, sent_y)
    each(REDUCERS, sent_z)
    each(NX - 1, lambda i: w_x(i + 1, x).wait_send())
    w_c.wait_send()

    @pl.when(reducing)
    def _():
        each(HALF - 1, lambda i: g_copy(low, i + 1).wait_send())

    final_c.wait_send()
    out_mine.wait()
    out_theirs.wait()
    for out in outs:
        out.wait()


def place(*refs):
    sources, outs, staged, sems = refs[:5], refs[5:10], refs[10:15], refs[15]
    pieces = [(2, pl.ds(i * 64, 64)) for i in range(4)]
    pieces += [(i, pl.ds(0, sources[i].shape[0])) for i in (0, 1, 3, 4)]
    loads = [
        pltpu.make_async_copy(sources[i].at[rows], staged[i].at[rows], sems.at[0, k])
        for k, (i, rows) in enumerate(pieces)
    ]
    stores = [
        pltpu.make_async_copy(staged[i].at[rows], outs[i].at[rows], sems.at[1, k])
        for k, (i, rows) in enumerate(pieces)
    ]
    for load in loads:
        load.start()
    for load, store in zip(loads, stores):
        load.wait()
        store.start()
    for store in stores:
        store.wait()


def on_device(tokens, key_cot, value_cot, key_mant, value_mant, key_expo, value_expo):
    dma = pltpu.SemaphoreType.DMA
    shape = jax.ShapeDtypeStruct
    anywhere = pl.BlockSpec(memory_space=pl.ANY)
    results = (
        shape((TOK, KVW), BF16),
        shape((TOK, KVW), BF16),
        shape((TOK, 2 * DH), BF16),
        shape((ROWS, KVW), F32),
        shape((ROWS, KVW), F32),
    )
    outs = pl.pallas_call(
        kernel,
        out_shape=results,
        in_specs=[anywhere] * 7,
        out_specs=(anywhere,) * 5,
        scratch_shapes=[
            pltpu.VMEM((TOK, 2 * DH), BF16),
            pltpu.VMEM((2, TOK, DH), BF16),
            pltpu.VMEM((2, TOK, KVW), BF16),
            pltpu.VMEM((TOK, KVW), BF16),
            pltpu.VMEM((2, ROWS, KVW), BF16),
            pltpu.VMEM((2, 2, ROWS), jnp.int32),
            pltpu.VMEM((2 * NY, NX, ROWS, KVW), F32),
            pltpu.VMEM((2, NX - 1, NY, ROWS, KVW), I16),
            pltpu.VMEM((2, NX - 1, NY, KVW), F32),
            pltpu.VMEM((2, NX - 1, NY, ROWS, KVW), I16),
            pltpu.VMEM((2, NX - 1, NY, KVW), F32),
            pltpu.VMEM((2, ROWS, KVW), F32),
            pltpu.VMEM((2, NY, ROWS, KVW), I16),
            pltpu.VMEM((2, NY, 1, KVW), F32),
            pltpu.VMEM((2, NY - 1, ROWS, KVW), I16),
            pltpu.VMEM((2, NY - 1, 1, KVW), F32),
            pltpu.VMEM((2, REDUCERS, 8, KVW), F32),
            pltpu.VMEM((NZ, 8, KVW), F32),
            pltpu.VMEM((2, ROWS, KVW), F32),
            pltpu.VMEM((NY, NX, ROWS, COLS), BF16),
            pltpu.VMEM((NY, NX, ROWS, COLS), BF16),
            pltpu.VMEM((2, TOK, DH), BF16),
            pltpu.VMEM((TOK, COLS), F32),
            pltpu.VMEM((TOK, COLS), BF16),
            dma((7,)),
            dma((6,)),
            dma((5,)), dma((5,)),
            dma((2, 2, NX - 1)), dma((2, 2, NX - 1)),
            dma((2, 2, NY - 1)), dma((2, 2, NY - 1)),
            dma((2, REDUCERS)), dma((NZ,)),
            dma((HALF - 1,)), dma((REDUCERS,)),
            pltpu.SemaphoreType.REGULAR,
            dma((3,)), dma,
            dma((NY - 1,)), dma((NY - 1,)),
            dma((NX - 1,)), dma((NX - 1,)),
        ],
        compiler_params=pltpu.CompilerParams(
            collective_id=0, has_side_effects=True, vmem_limit_bytes=64 * 1024 * 1024
        ),
        name="projections",
    )(tokens, key_cot, value_cot, key_mant, value_mant, key_expo.T, value_expo.T)
    return pl.pallas_call(
        place,
        out_shape=results,
        in_specs=[anywhere] * 5,
        out_specs=(anywhere,) * 5,
        scratch_shapes=[pltpu.VMEM(r.shape, r.dtype) for r in results] + [dma((2, 8))],
        compiler_params=pltpu.CompilerParams(vmem_limit_bytes=64 * 1024 * 1024),
        name="place",
    )(*outs)


def solution(mesh):
    rows, owned = P(("dp", "node"), None), P("node", None)
    return jax.shard_map(
        on_device,
        mesh=mesh,
        in_specs=(rows, rows, rows, owned, owned, owned, owned),
        out_specs=(rows, rows, rows, owned, owned),
        check_vma=False,
    )
```

```python
import math

import jax
import jax.numpy as jnp
from jax import lax
from jax.experimental import pallas as pl
from jax.experimental.pallas import tpu as pltpu
from jax.sharding import PartitionSpec as P

MESH = pl.DeviceIdType.MESH
F32, BF16, I16 = jnp.float32, jnp.bfloat16, jnp.int16
NX, NY, NZ = 4, 8, 12
HALF = NZ // 2
ROWS = 32
KVW = 256
COLS = 2 * KVW
TOK = 256
DH = 1024
REDUCERS = 4
STEPS = 32766.0
TINY = 1e-30


def coordinates():
    dp, node = lax.axis_index("dp"), lax.axis_index("node")
    x = lax.rem(node, NX)
    y = lax.rem(node // NX, NY)
    half = node // (NX * NY)
    low = dp // 2
    core = lax.rem(dp, 2)
    return x, y, half, low, core


def device(x, y, z, core):
    return {
        "dp": lax.rem(z, HALF) * 2 + core,
        "node": (z // HALF) * (NX * NY) + y * NX + x,
    }


def shard_rows(mant, expo_t):
    factor = jnp.zeros(expo_t.shape, F32)
    for exponent in range(-2, 2):
        factor = factor + jnp.where(expo_t == exponent, F32(2.0**exponent), F32(0.0))
    parts = []
    for block in range(2):
        spread = lax.dot_general(
            factor[block : block + 1, :],
            jnp.ones((1, 128), F32),
            (((0,), (0,)), ((), ())),
            preferred_element_type=F32,
        )
        parts.append(mant[:, block * 128 : (block + 1) * 128].astype(F32) * spread)
    return jnp.concatenate(parts, axis=1).astype(BF16)


def over_rows(left, right):
    return lax.dot_general(left, right, (((0,), (0,)), ((), ())), preferred_element_type=F32)


def over_cols(left, right):
    return lax.dot_general(left, right, (((1,), (1,)), ((), ())), preferred_element_type=F32)


def each(count, step):
    def body(i, _):
        step(i)
        return 0

    lax.fori_loop(0, count, body, 0)


def around(i, ring):
    return ring // 2 + (1 - 2 * lax.rem(i, 2)) * ((i + 1) // 2)


def kernel(
    tokens, key_cot, value_cot, key_mant, value_mant, key_expo, value_expo,
    keys, values, tokens_grad, key_grad, value_grad,
    tok, tok2, cot, cot2, mant, expo, part, codes, peaks, codes_in, peaks_in,
    sums, codes_y, peaks_y, codes_y_in, peaks_y_in, total, total_in, final, own_w, other_w, tgrad, kv, kv_out,
    load_sem, store_sem, send_c, recv_c, send_x, recv_x, send_y, recv_y,
    send_z, recv_z, send_g, recv_g, answered, send_wz, recv_wz, send_wy, recv_wy, send_wx, recv_wx,
):
    x, y, half, low, core = coordinates()
    z = half * HALF + low
    sibling = device(x, y, z, 1 - core)
    home = core == half

    def remote(src, dst, send, recv, to):
        return pltpu.make_async_remote_copy(
            src_ref=src, dst_ref=dst, send_sem=send, recv_sem=recv, device_id=to, device_id_type=MESH
        )

    loads = [
        pltpu.make_async_copy(key_mant, mant.at[0], load_sem.at[0]),
        pltpu.make_async_copy(value_mant, mant.at[1], load_sem.at[1]),
        pltpu.make_async_copy(key_expo, expo.at[0], load_sem.at[2]),
        pltpu.make_async_copy(value_expo, expo.at[1], load_sem.at[3]),
        pltpu.make_async_copy(tokens, tok, load_sem.at[4]),
        pltpu.make_async_copy(key_cot, cot.at[0], load_sem.at[5]),
        pltpu.make_async_copy(value_cot, cot.at[1], load_sem.at[6]),
    ]
    for load in loads[4:] + loads[:4]:
        load.start()

    barrier = pltpu.get_barrier_semaphore()

    def greet(to):
        pl.semaphore_signal(barrier, inc=1, device_id=to, device_id_type=MESH)

    each(NY - 1, lambda i: greet(device(x, lax.rem(y + around(i, NY), NY), z, core)))
    each(NX - 1, lambda i: greet(device(lax.rem(x + around(i, NX), NX), y, z, core)))
    greet(sibling)
    each(NZ - 1 - z, lambda i: greet(device(x, y, NZ - 1 - i, core)))

    for load in loads[4:]:
        load.wait()

    def own_part(b):
        left = tok[:, pl.ds(pl.multiple_of(b * 128, 128), 128)]
        return over_rows(left, cot[core]).reshape(NX, ROWS, KVW)

    def first_part(b, _):
        part[b] = own_part(b)
        return 0

    lax.fori_loop(0, NY, first_part, 0)
    pl.semaphore_wait(barrier, z + (NY - 1) + (NX - 1) + 1)
    each(
        z,
        lambda i: pl.semaphore_signal(
            answered, inc=1, device_id=device(x, y, i, core), device_id_type=MESH
        ),
    )

    def wait_answers():
        @pl.when(z < NZ - 1)
        def _():
            pl.semaphore_wait(answered, NZ - 1 - z)


    swap_cot = remote(cot.at[1 - core], cot2, send_c.at[0], recv_c.at[0], sibling)
    swaps = [
        remote(tok.at[:, pl.ds(h * DH, DH)], tok2.at[h], send_c.at[1 + h], recv_c.at[1 + h], sibling)
        for h in range(2)
    ]
    swap_cot.start()
    swaps[0].start()

    for load in loads[:4]:
        load.wait()

    @pl.when(home)
    def _():
        own_w[y, x, :, 0:KVW] = shard_rows(mant[0], expo[0])
        own_w[y, x, :, KVW:COLS] = shard_rows(mant[1], expo[1])

    edge = jnp.logical_or(low == 0, low == HALF - 1)
    outward = 2 * (low // (HALF - 1)) - 1

    def w_z(k):
        to = device(x, y, lax.rem(z + NZ + outward * k, NZ), core)
        return remote(own_w.at[y, x], own_w.at[y, x], send_wz.at[k - 1], recv_wz, to)

    def send_shard(of):
        @pl.when(jnp.logical_and(jnp.logical_and(home, edge), half == of))
        def _():
            each(HALF // 2, lambda i: w_z(HALF // 2 - i).start())

    send_shard(1)

    def x_copies(h, d):
        to = device(lax.rem(x + d, NX), y, z, core)
        return (
            remote(codes.at[h, d - 1], codes_in.at[h, d - 1],
                   send_x.at[0, h, d - 1], recv_x.at[0, h, d - 1], to),
            remote(peaks.at[h, d - 1], peaks_in.at[h, d - 1],
                   send_x.at[1, h, d - 1], recv_x.at[1, h, d - 1], to),
        )

    def coded(chunk):
        peak = jnp.maximum(jnp.max(jnp.abs(chunk), axis=0, keepdims=True), TINY)
        codes_of = jnp.round(chunk * (STEPS / peak)).astype(jnp.int32).astype(I16)
        return codes_of, peak * (1.0 / STEPS)

    def decoded(codes_of, scales):
        return codes_of.astype(jnp.int32).astype(F32) * scales

    swap_cot.wait_recv()
    for h in range(2):
        swaps[h].wait_recv()
        if h == 0:
            swaps[1].start()

        def both_parts(j, _, h=h):
            left = tok2[h, :, pl.ds(pl.multiple_of(j * 128, 128), 128)]
            b = h * NY + j
            first = part[b] if h == 0 else own_part(b)
            part[b] = first + over_rows(left, cot2[...]).reshape(NX, ROWS, KVW)
            return 0

        lax.fori_loop(0, NY, both_parts, 0)
        def encode_for(i, h=h):
            d = around(i, NX)

            def encode(j):
                codes[h, d - 1, j], scales = coded(part[h * NY + j, lax.rem(x + d, NX)])
                peaks[h, d - 1, pl.ds(j, 1), :] = scales

            each(NY, encode)
            if h == 0:
                for copy in x_copies(0, d):
                    copy.start()

        each(NX - 1, encode_for)

    @pl.when(edge)
    def _():
        wait_answers()

    send_shard(0)

    @pl.when(jnp.logical_not(home))
    def _():
        w_z(1).wait_recv()

    def w_y(d, block):
        to = device(x, lax.rem(y + d, NY), z, core)
        return remote(own_w.at[block, x], own_w.at[block, x], send_wy.at[d - 1], recv_wy.at[d - 1], to)

    each(NY - 1, lambda i: w_y(around(i, NY), y).start())

    def wait_sent_x(i, h):
        for copy in x_copies(h, i + 1):
            copy.wait_send()

    def start_x(i):
        for copy in x_copies(1, around(i, NX)):
            copy.start()

    each(NX - 1, lambda i: wait_sent_x(i, 0))
    each(NX - 1, start_x)

    def y_copies(h, d, block):
        to = device(x, lax.rem(y + d, NY), z, core)
        return (
            remote(codes_y.at[h, block], codes_y_in.at[h, d - 1],
                   send_y.at[0, h, d - 1], recv_y.at[0, h, d - 1], to),
            remote(peaks_y.at[h, block], peaks_y_in.at[h, d - 1],
                   send_y.at[1, h, d - 1], recv_y.at[1, h, d - 1], to),
        )

    def sum_x(h):
        def wait_x(i):
            for copy in x_copies(h, i + 1):
                copy.wait_recv()

        each(NX - 1, wait_x)

        def add_x(block):
            value = part[h * NY + block, x]
            for d in range(1, NX):
                value = value + decoded(codes_in[h, d - 1, block], peaks_in[h, d - 1, pl.ds(block, 1), :])
            return value

        def add_and_send(i):
            d = around(i, NY)
            block = lax.rem(y + d, NY)
            codes_y[h, block], peaks_y[h, block] = coded(add_x(block))
            for copy in y_copies(h, d, block):
                copy.start()

        each(NY - 1, add_and_send)
        sums[h] = add_x(y)

    sum_x(0)

    each(NX - 1, lambda i: wait_sent_x(i, 1))
    each(NY - 1, lambda i: w_y(i + 1, lax.rem(y + NY - 1 - i, NY)).wait_recv())

    def w_x(d, column):
        to = device(lax.rem(x + d, NX), y, z, core)
        return remote(own_w.at[:, column], own_w.at[:, column], send_wx.at[d - 1], recv_wx.at[d - 1], to)

    each(NX - 1, lambda i: w_x(around(i, NX), x).start())

    scale = F32(1.0 / math.sqrt(NX * NY * NZ * 2 * TOK))
    reducing = low < REDUCERS

    def z_copy(h, j, slot):
        to = device(x, y, h * HALF + j, core)
        return remote(total.at[h, j], total_in.at[slot], send_z.at[h, j], recv_z.at[slot], to)

    def rows_of(j):
        return pl.ds(pl.multiple_of(8 * j, 8), 8)

    def g_copy(row, d):
        to = device(x, y, half * HALF + lax.rem(low + d, HALF), core)
        rows = final.at[core, rows_of(row)]
        return remote(rows, rows, send_g.at[d - 1], recv_g.at[row], to)

    def send_sums(h):
        def wait_y(i):
            for copy in y_copies(h, i + 1, y):
                copy.wait_recv()

        each(NY - 1, wait_y)
        value = sums[h]
        for d in range(1, NY):
            value = value + decoded(codes_y_in[h, d - 1], peaks_y_in[h, d - 1])
        total[h] = value.reshape(REDUCERS, 8, KVW)

        def send(j):
            @pl.when(z != h * HALF + j)
            def _():
                z_copy(h, j, z).start()

        each(REDUCERS, send)

    def reduce_sums(h):
        @pl.when(jnp.logical_and(half == h, reducing))
        def _():
            each(NZ - 1, lambda i: z_copy(h, 0, lax.rem(z + i + 1, NZ)).wait_recv())
            value = total[h, low]
            for d in range(1, NZ):
                value = value + total_in[lax.rem(z + d, NZ)]
            final[core, rows_of(low), :] = value * scale
            each(HALF - 1, lambda i: g_copy(low, around(i, HALF)).start())

    @pl.when(jnp.logical_not(edge))
    def _():
        wait_answers()

    send_sums(0)
    sum_x(1)
    send_sums(1)

    each(NX - 1, lambda i: w_x(i + 1, lax.rem(x + NX - 1 - i, NX)).wait_recv())
    w_c = remote(own_w, other_w, send_c.at[3], recv_c.at[3], sibling)
    w_c.start()
    reduce_sums(0)

    def products(weights, which, first):
        def tile(t):
            rows = weights[pl.ds(t * 2, 2)].reshape(256, COLS)
            at = pl.ds(pl.multiple_of(t * 256, 256), 256)
            grad = over_cols(cot[0], rows[:, 0:KVW]) + over_cols(cot[1], rows[:, KVW:COLS])
            tgrad[which, :, at] = grad.astype(BF16)
            left = tok[:, pl.ds(pl.multiple_of(which * DH + t * 256, 256), 256)]
            kv[...] = kv[...] + jnp.dot(left, rows, preferred_element_type=F32)

        if first:
            kv[...] = jnp.zeros_like(kv)
        each(NY // 2, tile)
        columns = pl.ds(pl.multiple_of(which * DH, DH), DH)
        out = pltpu.make_async_copy(tgrad.at[which], tokens_grad.at[:, columns], store_sem.at[0 if first else 1])
        out.start()
        return out

    out_mine = products(own_w, core, True)
    reduce_sums(1)
    w_c.wait_recv()
    out_theirs = products(other_w, 1 - core, False)
    kv_out[...] = kv[...].astype(BF16)
    outs = [
        pltpu.make_async_copy(kv_out.at[:, pl.ds(0, KVW)], keys, store_sem.at[2]),
        pltpu.make_async_copy(kv_out.at[:, pl.ds(KVW, KVW)], values, store_sem.at[3]),
    ]
    for out in outs:
        out.start()

    def wait_rows(j):
        @pl.when(low != j)
        def _():
            g_copy(j, 1).wait_recv()

    each(REDUCERS, wait_rows)

    final_c = remote(final.at[core], final.at[core], send_c.at[4], recv_c.at[4], sibling)
    final_c.start()
    remote(final.at[1 - core], final.at[1 - core], send_c.at[4], recv_c.at[4], sibling).wait_recv()
    outs += [
        pltpu.make_async_copy(final.at[0], key_grad, store_sem.at[4]),
        pltpu.make_async_copy(final.at[1], value_grad, store_sem.at[5]),
    ]
    for out in outs[2:]:
        out.start()

    swap_cot.wait_send()
    for swap in swaps:
        swap.wait_send()

    @pl.when(jnp.logical_and(home, edge))
    def _():
        each(HALF // 2, lambda i: w_z(i + 1).wait_send())

    def sent_y(i):
        for h in range(2):
            for copy in y_copies(h, i + 1, y):
                copy.wait_send()
        w_y(i + 1, y).wait_send()

    def sent_z(j):
        for h in range(2):

            @pl.when(z != h * HALF + j)
            def _(h=h):
                z_copy(h, j, z).wait_send()

    each(NY - 1, sent_y)
    each(REDUCERS, sent_z)
    each(NX - 1, lambda i: w_x(i + 1, x).wait_send())
    w_c.wait_send()

    @pl.when(reducing)
    def _():
        each(HALF - 1, lambda i: g_copy(low, i + 1).wait_send())

    final_c.wait_send()
    out_mine.wait()
    out_theirs.wait()
    for out in outs:
        out.wait()


def place(*refs):
    sources, outs, staged, sems = refs[:5], refs[5:10], refs[10:15], refs[15]
    pieces = [(2, pl.ds(i * 64, 64)) for i in range(4)]
    pieces += [(i, pl.ds(0, sources[i].shape[0])) for i in (0, 1, 3, 4)]
    loads = [
        pltpu.make_async_copy(sources[i].at[rows], staged[i].at[rows], sems.at[0, k])
        for k, (i, rows) in enumerate(pieces)
    ]
    stores = [
        pltpu.make_async_copy(staged[i].at[rows], outs[i].at[rows], sems.at[1, k])
        for k, (i, rows) in enumerate(pieces)
    ]
    for load in loads:
        load.start()
    for load, store in zip(loads, stores):
        load.wait()
        store.start()
    for store in stores:
        store.wait()


def on_device(tokens, key_cot, value_cot, key_mant, value_mant, key_expo, value_expo):
    dma = pltpu.SemaphoreType.DMA
    shape = jax.ShapeDtypeStruct
    anywhere = pl.BlockSpec(memory_space=pl.ANY)
    results = (
        shape((TOK, KVW), BF16),
        shape((TOK, KVW), BF16),
        shape((TOK, 2 * DH), BF16),
        shape((ROWS, KVW), F32),
        shape((ROWS, KVW), F32),
    )
    outs = pl.pallas_call(
        kernel,
        out_shape=results,
        in_specs=[anywhere] * 7,
        out_specs=(anywhere,) * 5,
        scratch_shapes=[
            pltpu.VMEM((TOK, 2 * DH), BF16),
            pltpu.VMEM((2, TOK, DH), BF16),
            pltpu.VMEM((2, TOK, KVW), BF16),
            pltpu.VMEM((TOK, KVW), BF16),
            pltpu.VMEM((2, ROWS, KVW), BF16),
            pltpu.VMEM((2, 2, ROWS), jnp.int32),
            pltpu.VMEM((2 * NY, NX, ROWS, KVW), F32),
            pltpu.VMEM((2, NX - 1, NY, ROWS, KVW), I16),
            pltpu.VMEM((2, NX - 1, NY, KVW), F32),
            pltpu.VMEM((2, NX - 1, NY, ROWS, KVW), I16),
            pltpu.VMEM((2, NX - 1, NY, KVW), F32),
            pltpu.VMEM((2, ROWS, KVW), F32),
            pltpu.VMEM((2, NY, ROWS, KVW), I16),
            pltpu.VMEM((2, NY, 1, KVW), F32),
            pltpu.VMEM((2, NY - 1, ROWS, KVW), I16),
            pltpu.VMEM((2, NY - 1, 1, KVW), F32),
            pltpu.VMEM((2, REDUCERS, 8, KVW), F32),
            pltpu.VMEM((NZ, 8, KVW), F32),
            pltpu.VMEM((2, ROWS, KVW), F32),
            pltpu.VMEM((NY, NX, ROWS, COLS), BF16),
            pltpu.VMEM((NY, NX, ROWS, COLS), BF16),
            pltpu.VMEM((2, TOK, DH), BF16),
            pltpu.VMEM((TOK, COLS), F32),
            pltpu.VMEM((TOK, COLS), BF16),
            dma((7,)),
            dma((6,)),
            dma((5,)), dma((5,)),
            dma((2, 2, NX - 1)), dma((2, 2, NX - 1)),
            dma((2, 2, NY - 1)), dma((2, 2, NY - 1)),
            dma((2, REDUCERS)), dma((NZ,)),
            dma((HALF - 1,)), dma((REDUCERS,)),
            pltpu.SemaphoreType.REGULAR,
            dma((3,)), dma,
            dma((NY - 1,)), dma((NY - 1,)),
            dma((NX - 1,)), dma((NX - 1,)),
        ],
        compiler_params=pltpu.CompilerParams(
            collective_id=0, has_side_effects=True, vmem_limit_bytes=64 * 1024 * 1024
        ),
        name="projections",
    )(tokens, key_cot, value_cot, key_mant, value_mant, key_expo.T, value_expo.T)
    return pl.pallas_call(
        place,
        out_shape=results,
        in_specs=[anywhere] * 5,
        out_specs=(anywhere,) * 5,
        scratch_shapes=[pltpu.VMEM(r.shape, r.dtype) for r in results] + [dma((2, 8))],
        compiler_params=pltpu.CompilerParams(vmem_limit_bytes=64 * 1024 * 1024),
        name="place",
    )(*outs)


def solution(mesh):
    rows, owned = P(("dp", "node"), None), P("node", None)
    return jax.shard_map(
        on_device,
        mesh=mesh,
        in_specs=(rows, rows, rows, owned, owned, owned, owned),
        out_specs=(rows, rows, rows, owned, owned),
        check_vma=False,
    )
```
